256 devices in a mesh: leaf: 64 (over z, y, core), rhs: 4 (over x).
Axes of the slice: x: 4, y: 4, z: 8, core: 2. Of those that a mesh axis runs over, the one named last changes fastest.
Arguments:
- targets: float32 [16, 524288], P('rhs', 'leaf'), may hold values from -6 to 6
- points: float32 [8, 524288], P(None, 'leaf'), may hold values from -5 to 5
- tree_order: int32 [524288], P('leaf'), may hold values from 0 to 8191, as said below
- leaf_basis: bfloat16 [2048, 256, 128], P('leaf'), may hold values from -0.375 to 0.375
- transfer_local: bfloat16 [1984, 256, 128], P('leaf'), may hold values from -0.375 to 0.375
- coupling_local: bfloat16 [1984, 128, 128], P('leaf'), may hold values from -0.25 to 0.25
- transfer_top: bfloat16 [63, 256, 128], P(None, None, 'rhs'), may hold values from -0.375 to 0.375
- coupling_top: bfloat16 [63, 128, 128], P(None, None, 'rhs'), may hold values from -0.25 to 0.25
Outputs:
- solution_out: float32 [16, 524288], P('rhs', 'leaf')
- residual_out: float32 [16, 524288], P('rhs', 'leaf')
The draws below stay inside these ranges and needn't reach their ends.
Inputs may be any that keep to these rules, and one draw needn't show every extreme that they name: `tree_order`: each aligned block of 8192 entries is a permutation of 0 to 8191.
All inputs are finite; a program needn't handle non-finite values.
Results may differ from the reference program's by a relative error of at most 0.011.
Values may be sent and summed in bfloat16 or wider, within the bound.
A program may use at most 128 MiB of HBM per device.

```python
import jax
import jax.numpy as jnp
from jax import lax

RANK = 128
LEAF = 256
DIMS = 8
NRHS = 16
ITERS = 2
LEAF_DEV = 32
NP_DEV = 8192
NPTS = 524288
LEAVES = 2048
LOCAL_NODES = 1984
TOP_NODES = 63
N_LEAF = 64


def draw_tree_order(key, part):
    key = jax.random.fold_in(key, 11)
    subkeys = jax.random.split(key, NPTS // NP_DEV)
    blocks = jax.vmap(lambda subkey: jax.random.permutation(subkey, NP_DEV))(subkeys)
    return blocks.reshape(NPTS).astype(jnp.int32)


def level_of(rng, dims, shards, smallest, largest):
    level, own = 1.0, jax.random.fold_in(rng, 6)
    for dim, parts in shards:
        steps = jnp.exp(jax.random.uniform(jax.random.fold_in(own, dim), (parts,), jnp.float32, smallest / len(shards), largest / len(shards)))
        level = level * jnp.repeat(steps, dims[dim] // parts).reshape([-1 if axis == dim else 1 for axis in range(len(dims))])
    return level


def gaussian(own_key, extent, scale, limit, shards=(), held_as=jnp.bfloat16):
    values = jax.random.normal(own_key, extent, jnp.float32) * scale
    if len(shards) > 0:
        values = level_of(own_key, extent, shards, -0.22, 0.18) * values
    return jnp.clip(values, min=-limit, max=limit).astype(held_as)


def setup_inputs(seed: int = 0) -> dict:
    splits = jax.random.split(jax.random.key(seed), 9)
    targets = gaussian(splits[0], (NRHS, NPTS), 1.0, 6.0, ((0, 4), (1, 64)), jnp.float32)
    points = gaussian(splits[1], (DIMS, NPTS), 1.0, 5.0, ((1, 64),), jnp.float32)
    tree_order = draw_tree_order(jax.random.fold_in(splits[8], 71), 0)
    leaf_basis = gaussian(splits[3], (LEAVES, LEAF, RANK), LEAF ** -0.5, 0.375, ((0, 64),))
    transfer_local = gaussian(splits[4], (LOCAL_NODES, 2 * RANK, RANK), (2 * RANK) ** -0.5, 0.375, ((0, 64),))
    coupling_local = gaussian(splits[5], (LOCAL_NODES, RANK, RANK), (4 * RANK) ** -0.5, 0.25, ((0, 64),))
    transfer_top = gaussian(splits[6], (TOP_NODES, 2 * RANK, RANK), (2 * RANK) ** -0.5, 0.375, ((2, 4),))
    coupling_top = gaussian(splits[7], (TOP_NODES, RANK, RANK), (4 * RANK) ** -0.5, 0.25, ((2, 4),))
    return dict(targets=targets, points=points, tree_order=tree_order, leaf_basis=leaf_basis, transfer_local=transfer_local, coupling_local=coupling_local, transfer_top=transfer_top, coupling_top=coupling_top)


exact_mode = lax.Precision.HIGHEST
kernel_rate = 0.0625
ridge_term = 1.0


def rounded(values):
    return lax.optimization_barrier(values.astype(jnp.bfloat16)).astype(jnp.float32)


def kernel_apply(pts_tree, vector):
    columns = vector.shape[0]
    blocks = vector.shape[1] // LEAF
    spots = jnp.moveaxis(pts_tree.reshape(DIMS, blocks, LEAF), 1, 0)
    values = jnp.moveaxis(vector.reshape(columns, blocks, LEAF), 1, 0)

    def one_leaf(pieces):
        spot, value = pieces
        spread = spot[:, :, None] - spot[:, None, :]
        kernel = jnp.exp(-kernel_rate * jnp.sum(spread * spread, axis=0))
        return jnp.dot(value, kernel, precision=exact_mode, preferred_element_type=jnp.float32) + ridge_term * value

    result = lax.map(one_leaf, (spots, values))
    return jnp.moveaxis(result, 0, 1).reshape(columns, -1)


def climb(coeffs, transfer):
    groups, number, columns, rank = coeffs.shape
    saved = []
    offset = 0
    while number > 1:
        halves = number // 2
        paired = coeffs.reshape(groups, halves, 2, columns, rank)
        joined = jnp.concatenate([paired[:, :, 0], paired[:, :, 1]], axis=-1)
        matrices = transfer[:, offset:offset + halves].astype(jnp.float32)
        coeffs = rounded(jnp.einsum("ghcq,ghqr->ghcr", joined, matrices, precision=exact_mode))
        saved.append((paired, offset, halves))
        offset += halves
        number = halves
    return coeffs[:, 0], saved


def descend(root_field, saved, transfer, coupling):
    groups, columns, rank = root_field.shape
    field = root_field[:, None]
    for paired, offset, halves in reversed(saved):
        matrices = transfer[:, offset:offset + halves].astype(jnp.float32).reshape(groups, halves, 2, rank, rank)
        links = coupling[:, offset:offset + halves].astype(jnp.float32)
        child = jnp.einsum("ghcb,ghsab->ghsca", rounded(field), matrices, precision=exact_mode)
        toward_left = jnp.einsum("ghcb,ghab->ghca", paired[:, :, 1], links, precision=exact_mode)
        toward_right = jnp.einsum("ghca,ghab->ghcb", paired[:, :, 0], links, precision=exact_mode)
        field = (child + jnp.stack([toward_left, toward_right], axis=2)).reshape(groups, 2 * halves, columns, rank)
    return field


def apply_matrix(direction, pts_tree, leaf_basis, transfer_local, coupling_local, transfer_top, coupling_top):
    dense = kernel_apply(pts_tree, direction)
    groups = N_LEAF
    basis = leaf_basis.astype(jnp.float32).reshape(groups, LEAF_DEV, LEAF, RANK)
    values = rounded(direction).reshape(NRHS, groups, LEAF_DEV, LEAF)
    coeffs = rounded(jnp.einsum("cgla,glar->glcr", values, basis, precision=exact_mode))
    local_transfer = transfer_local.reshape(groups, LEAF_DEV - 1, 2 * RANK, RANK)
    local_coupling = coupling_local.reshape(groups, LEAF_DEV - 1, RANK, RANK)
    roots, saved_local = climb(coeffs, local_transfer)
    summit, saved_top = climb(roots[None], transfer_top[None])
    top_field = descend(jnp.zeros_like(summit), saved_top, transfer_top[None], coupling_top[None])[0]
    fields = descend(top_field, saved_local, local_transfer, local_coupling)
    lowrank = jnp.einsum("glcr,glar->cgla", rounded(fields), basis, precision=exact_mode).reshape(NRHS, NPTS)
    return dense + lowrank


def reference(targets, points, tree_order, leaf_basis, transfer_local, coupling_local, transfer_top, coupling_top):
    positions = (tree_order + (jnp.arange(NPTS, dtype=jnp.int32) // NP_DEV) * NP_DEV).astype(jnp.int32)
    start = targets[:, positions]
    pts_tree = points[:, positions]
    solution = jnp.zeros_like(start)
    residual = start
    direction = start
    norm_now = jnp.sum(residual * residual, axis=1)
    for repeat in range(ITERS):
        product_vec = apply_matrix(direction, pts_tree, leaf_basis, transfer_local, coupling_local, transfer_top, coupling_top)
        step_size = norm_now / jnp.sum(direction * product_vec, axis=1)
        solution = solution + step_size[:, None] * direction
        residual = residual - step_size[:, None] * product_vec
        norm_next = jnp.sum(residual * residual, axis=1)
        direction = residual + (norm_next / norm_now)[:, None] * direction
        norm_now = norm_next
    solution_out = jnp.zeros_like(start).at[:, positions].set(solution)
    residual_out = jnp.zeros_like(start).at[:, positions].set(residual)
    return solution_out, residual_out
```

```python
import functools

import jax
import jax.numpy as jnp
from jax import lax
from jax.experimental import pallas as pl
from jax.experimental.pallas import tpu as pltpu
from jax.sharding import PartitionSpec as P

LEAF = 256
RANK = 128
DIMS = 8
ROWS = 8
kernel_rate = 0.0625
ridge_term = 1.0

f32 = jnp.float32
bf16 = jnp.bfloat16
MESH = pl.DeviceIdType.MESH
ROUNDS = 8


def rounded(values):
    return values.astype(bf16).astype(f32)


def batched(left, right):
    return lax.dot_general(left, right, (((2,), (1,)), ((0,), (0,))), preferred_element_type=f32)


def batched_t(left, right):
    return lax.dot_general(left, right, (((2,), (2,)), ((0,), (0,))), preferred_element_type=f32)


def up_level(coeffs, matrices, multiply=batched):
    half = coeffs.shape[0] // 2
    paired = coeffs.reshape(half, 2, ROWS, RANK)
    joined = jnp.concatenate([paired[:, 0], paired[:, 1]], axis=-1).astype(bf16)
    return rounded(multiply(joined, matrices)), paired


def whole_kernel(
    sizes,
    tgt_ref,
    pts_ref,
    idx_ref,
    basis_hbm,
    transfer_hbm,
    coupling_hbm,
    ttop_hbm,
    ctop_hbm,
    sol_ref,
    res_ref,
    basis,
    transfer,
    coupling,
    top_t,
    top_c,
    lhs_t32,
    lhs_t,
    lhs_p,
    onehot,
    k_high,
    k_low,
    vec,
    dense,
    image,
    first,
    acc,
    links,
    slots,
    load_sem,
    x_send,
    x_recv,
    t_send,
    t_recv,
):
    spread, group, planes, leaves = sizes
    leaf = lax.axis_index("leaf")
    mine = lax.axis_index("rhs")
    inner = lax.rem(leaf, group)
    plane = leaf // group
    base = plane * group

    barrier = pltpu.get_barrier_semaphore()

    def greet_inner(j, carry):
        other = base + lax.rem(inner + j, group)
        pl.semaphore_signal(barrier, inc=1, device_id=(other, mine), device_id_type=MESH)
        return carry

    def greet_plane(j, carry):
        other = inner + group * lax.rem(plane + j, planes)
        pl.semaphore_signal(barrier, inc=1, device_id=(other, mine), device_id_type=MESH)
        return carry

    def greet_x(j, carry):
        other = lax.rem(mine + j, spread)
        pl.semaphore_signal(barrier, inc=1, device_id=(leaf, other), device_id_type=MESH)
        return carry

    lax.fori_loop(1, group, greet_inner, 0)
    lax.fori_loop(1, planes, greet_plane, 0)
    lax.fori_loop(1, spread, greet_x, 0)

    width = RANK // spread
    mine_rows = pl.ds(pl.multiple_of(mine * width, width), width)
    tops = []
    low_levels = group.bit_length() - 1
    high_levels = planes.bit_length() - 1
    count = group * planes
    place = 0
    first_node = 0
    for level in range(low_levels):
        here = group >> level + 1
        tops.append((first_node + plane * here, place, here))
        place += here
        first_node += count >> level + 1
    tops.append((first_node, place, planes - 1))
    place += planes - 1
    nodes = place
    top_loads = []
    for i, (source, target, number) in enumerate(tops):
        for hbm, top, k in ((ttop_hbm, top_t, 0), (ctop_hbm, top_c, 1)):
            copy = pltpu.make_async_copy(
                hbm.at[pl.ds(source, number)],
                top.at[pl.ds(target, number), mine_rows],
                load_sem.at[3 + 2 * i + k],
            )
            copy.start()
            top_loads.append(copy)
    load_basis = pltpu.make_async_copy(basis_hbm, basis, load_sem.at[0])
    load_transfer = pltpu.make_async_copy(transfer_hbm, transfer, load_sem.at[1])
    load_coupling = pltpu.make_async_copy(coupling_hbm, coupling, load_sem.at[2])
    load_basis.start()
    load_transfer.start()
    load_coupling.start()
    pl.semaphore_wait(barrier, group - 1 + planes - 1 + spread - 1)

    def x_copies(owner, j, other):
        own_rows = pl.ds(pl.multiple_of(owner * width, width), width)
        return [
            pltpu.make_async_remote_copy(
                src_ref=top.at[:, own_rows],
                dst_ref=top.at[:, own_rows],
                send_sem=x_send.at[k, j - 1],
                recv_sem=x_recv.at[k, owner],
                device_id=(leaf, other),
                device_id_type=MESH,
            )
            for k, top in enumerate((top_t, top_c))
        ]

    for copy in top_loads:
        copy.wait()

    def x_start(j, carry):
        for copy in x_copies(mine, j, lax.rem(mine + j, spread)):
            copy.start()
        return carry

    lax.fori_loop(1, spread, x_start, 0)

    def tile_copy(turn, slot, j, other):
        return pltpu.make_async_remote_copy(
            src_ref=slots.at[turn, slot],
            dst_ref=slots.at[turn, slot],
            send_sem=t_send.at[turn, j - 1],
            recv_sem=t_recv.at[turn, slot],
            device_id=(other, mine),
            device_id_type=MESH,
        )

    def partner(turn, j):
        if turn % 2 == 0:
            slot = lax.rem(inner + j, group)
            return slot, base + slot
        slot = lax.rem(plane + j, planes)
        return slot, inner + group * slot

    def exchange_start(turn, tile):
        me, number = (inner, group) if turn % 2 == 0 else (plane, planes)
        slots[turn, me] = tile

        def step(j, carry):
            tile_copy(turn, me, j, partner(turn, j)[1]).start()
            return carry

        lax.fori_loop(1, number, step, 0)

    def exchange_wait(turn):
        number = group if turn % 2 == 0 else planes

        def step(j, carry):
            slot, other = partner(turn, j)
            tile_copy(turn, slot, j, other).wait_recv()
            return carry

        lax.fori_loop(1, number, step, 0)
        return slots[turn, :number]

    for h in range(leaves):
        piece = tgt_ref[:, h * LEAF : (h + 1) * LEAF]
        high = rounded(piece)
        lhs_t32[h * 8 : h * 8 + 4, :] = high
        lhs_t32[h * 8 + 4 : h * 8 + 8, :] = piece - high
        piece = pts_ref[:, h * LEAF : (h + 1) * LEAF]
        high = rounded(piece)
        lhs_p[h * 16 : (h + 1) * 16, :] = jnp.concatenate([high, piece - high], axis=0).astype(bf16)
    lhs_t[...] = lhs_t32[...].astype(bf16)

    def index_row(c):
        return jnp.concatenate(
            [idx_ref[pl.ds(2 * c, 1), :], idx_ref[pl.ds(2 * c + 1, 1), :]], axis=1
        )

    def gather_leaf(c, carry):
        order = index_row(c)
        low = lax.bitwise_and(order, LEAF - 1)
        high = lax.shift_right_logical(order, 8)
        hot = lax.broadcasted_iota(jnp.int32, (LEAF, LEAF), 0) == low
        hot = jnp.where(hot, 1.0, 0.0).astype(bf16)
        onehot[c] = hot
        rows_t = jnp.dot(lhs_t[...], hot, preferred_element_type=f32).reshape(leaves, 8, LEAF)
        rows_p = jnp.dot(lhs_p[...], hot, preferred_element_type=f32).reshape(leaves, 16, LEAF)
        here_t = lax.broadcasted_iota(jnp.int32, (leaves, 8, LEAF), 0) == high[None]
        here_p = lax.broadcasted_iota(jnp.int32, (leaves, 16, LEAF), 0) == high[None]
        both = jnp.sum(jnp.where(here_t, rows_t, 0.0), axis=0)
        spots = jnp.sum(jnp.where(here_p, rows_p, 0.0), axis=0)
        vec[c] = both + pltpu.roll(both, 4, 0)
        spot_high, spot_low = spots[:8], spots[8:]
        whole = spot_high + spot_low
        norm = jnp.sum(whole * whole, axis=0, keepdims=True) * -kernel_rate
        norm_a = rounded(norm)
        norm_b = rounded(norm - norm_a)
        norm_c = norm - norm_a - norm_b
        row = lax.broadcasted_iota(jnp.int32, (8, LEAF), 0)
        norms = jnp.where(row == 0, norm_a, jnp.where(row == 1, norm_b, norm_c))
        ones = jnp.ones((8, LEAF), f32)
        zeros = jnp.zeros((8, LEAF), f32)
        tail_left = jnp.where(row < 3, norms, jnp.where(row < 6, ones, zeros))
        norms_up = jnp.where(row == 3, norm_a, jnp.where(row == 4, norm_b, norm_c))
        tail_right = jnp.where(row < 3, ones, jnp.where(row < 6, norms_up, zeros))
        left = jnp.concatenate(
            [spot_high, spot_high, spot_low, spot_low, tail_left, zeros], axis=0
        ).astype(bf16)
        right_high = spot_high * (2 * kernel_rate)
        right_low = spot_low * (2 * kernel_rate)
        right = jnp.concatenate(
            [right_high, right_low, right_high, right_low, tail_right, zeros], axis=0
        ).astype(bf16)
        power = lax.dot_general(left, right, (((0,), (0,)), ((), ())), preferred_element_type=f32)
        values = jnp.exp(power)
        values_high = values.astype(bf16)
        k_high[c] = values_high
        k_low[c] = (values - values_high.astype(f32)).astype(bf16)
        return carry

    lax.fori_loop(0, leaves, gather_leaf, 0)

    def x_wait(j, carry):
        other = lax.rem(mine + j, spread)
        for copy in x_copies(other, j, other):
            copy.wait_recv()
        return carry

    lax.fori_loop(1, spread, x_wait, 0)

    row8 = lax.broadcasted_iota(jnp.int32, (ROWS, RANK), 0)
    upper = row8 < 4

    def swap(tile):
        return pltpu.roll(tile, 4, 0)

    def lane_partial(product):
        total = jnp.sum(product, axis=0)
        return total[:, :RANK] + total[:, RANK:]

    def full(tile):
        return jnp.broadcast_to(jnp.sum(tile, axis=1, keepdims=True), (ROWS, RANK))

    def wide_of(tile):
        return jnp.concatenate([tile, tile], axis=1)[None]

    def apply_matrix(turn):
        value = vec[...]
        square = lane_partial(value * value)
        coeffs = rounded(batched(value.astype(bf16), basis[...]))
        saved = []
        offset = 0
        number = leaves
        while number > 1:
            half = number // 2
            coeffs, paired = up_level(coeffs, transfer[offset : offset + half])
            saved.append((paired, offset, half))
            offset += half
            number = half
        exchange_start(turn, jnp.where(upper, coeffs[0], square))

        high = rounded(value)
        sub_row = lax.broadcasted_iota(jnp.int32, value.shape, 1)
        stacked = jnp.where(sub_row < 4, high, value - high).astype(bf16)
        product = batched(stacked, k_high[...]) + batched(stacked, k_low[...])
        dense[...] = product + pltpu.roll(product, 4, 1) + ridge_term * value

        tiles = exchange_wait(turn)
        group_square = jnp.sum(tiles, axis=0)
        levels = [tiles]
        place = 0
        while levels[-1].shape[0] > 1:
            half = levels[-1].shape[0] // 2
            levels.append(up_level(levels[-1], top_t[place : place + half], batched_t)[0])
            place += half
        exchange_start(turn + 1, jnp.where(upper, levels.pop()[0], group_square))

        for paired, offset, half in saved:
            matrices = coupling[offset : offset + half]
            links[0, offset : offset + half] = batched_t(paired[:, 1].astype(bf16), matrices)
            links[1, offset : offset + half] = batched(paired[:, 0].astype(bf16), matrices)

        tiles = exchange_wait(turn + 1)
        total_square = jnp.sum(tiles, axis=0)
        levels.append(tiles)
        while levels[-1].shape[0] > 2:
            half = levels[-1].shape[0] // 2
            levels.append(up_level(levels[-1], top_t[place : place + half], batched_t)[0])
            place += half

        field = None
        place = nodes
        for level in reversed(range(low_levels + high_levels)):
            if level >= low_levels:
                number = planes >> level - low_levels + 1
            else:
                number = group >> level + 1
            place -= number
            spot = plane if level >= low_levels else inner
            depth = level - low_levels if level >= low_levels else level
            node = lax.shift_right_logical(spot, depth + 1)
            side = lax.bitwise_and(lax.shift_right_logical(spot, depth), 1)
            pairs = levels[level]
            sibling = jnp.zeros((ROWS, RANK), f32)
            for k in range(pairs.shape[0]):
                chosen = lax.shift_right_logical(spot, depth) + 1 - 2 * side == k
                sibling = jnp.where(chosen, pairs[k], sibling)
            sibling = sibling.astype(bf16)
            link = top_c[place + node]
            to_left = jnp.dot(sibling, link, preferred_element_type=f32)
            to_right = lax.dot_general(
                sibling, link, (((1,), (1,)), ((), ())), preferred_element_type=f32
            )
            own = jnp.where(side == 0, to_left, to_right)
            if field is not None:
                half_lanes = pl.multiple_of(side * RANK, RANK)
                half = top_t[place + node, :, pl.ds(half_lanes, RANK)]
                own = own + jnp.dot(field.astype(bf16), half, preferred_element_type=f32)
            field = own
        field = jnp.where(upper, field, swap(field))[None]

        for _, offset, half in reversed(saved):
            child = batched_t(field.astype(bf16), transfer[offset : offset + half])
            left = child[:, :, :RANK] + links[0, offset : offset + half]
            right = child[:, :, RANK:] + links[1, offset : offset + half]
            field = jnp.stack([left, right], axis=1).reshape(2 * half, ROWS, RANK)
        image[...] = dense[...] + batched_t(field.astype(bf16), basis[...])
        total_square = full(total_square)
        return jnp.where(upper, swap(total_square), total_square)

    def reduce_all(turn, partial):
        exchange_start(turn, partial)
        total = jnp.sum(exchange_wait(turn), axis=0)
        exchange_start(turn + 1, total)
        return full(jnp.sum(exchange_wait(turn + 1), axis=0))

    load_basis.wait()
    load_transfer.wait()
    load_coupling.wait()

    rr_first = apply_matrix(0)
    start = vec[...]
    step_size = rr_first / reduce_all(2, lane_partial(start * image[...]))
    first[0] = start
    first[1] = image[...]
    vec[...] = start - wide_of(step_size) * image[...]

    rr_second = apply_matrix(4)
    ratio = wide_of(rr_second / rr_first)
    residual = vec[...]
    direction = residual + ratio * first[0]
    image[...] = image[...] + ratio * first[1]
    last_size = rr_second / reduce_all(6, lane_partial(direction * image[...]))
    solution = wide_of(step_size) * first[0] + wide_of(last_size) * direction
    residual = residual - wide_of(last_size) * image[...]
    sub_row = lax.broadcasted_iota(jnp.int32, residual.shape, 1)
    vec[...] = jnp.where(sub_row < 4, solution, residual)

    acc[...] = jnp.zeros_like(acc)

    def scatter_leaf(c, carry):
        order = index_row(c)
        high = lax.shift_right_logical(order, 8)
        here = lax.broadcasted_iota(jnp.int32, (leaves, 8, LEAF), 0) == high[None]
        value = vec[c]
        value_high = rounded(value)
        value_low = value - value_high
        part_high = jnp.where(here, value_high[None], 0.0).reshape(leaves * 8, LEAF)
        part_low = jnp.where(here, value_low[None], 0.0).reshape(leaves * 8, LEAF)
        rows = jnp.concatenate([part_high, part_low], axis=0).astype(bf16)
        acc[...] += lax.dot_general(
            rows, onehot[c], (((1,), (1,)), ((), ())), preferred_element_type=f32
        )
        return carry

    lax.fori_loop(0, leaves, scatter_leaf, 0)
    for h in range(leaves):
        tile = acc[h * 8 : h * 8 + 8, :] + acc[leaves * 8 + h * 8 : leaves * 8 + h * 8 + 8, :]
        sol_ref[:, h * LEAF : (h + 1) * LEAF] = tile[:4]
        res_ref[:, h * LEAF : (h + 1) * LEAF] = tile[4:]

    def x_done(j, carry):
        for copy in x_copies(mine, j, lax.rem(mine + j, spread)):
            copy.wait_send()
        return carry

    lax.fori_loop(1, spread, x_done, 0)
    for turn in range(ROUNDS):
        me, number = (inner, group) if turn % 2 == 0 else (plane, planes)

        def sent(j, carry):
            tile_copy(turn, me, j, partner(turn, j)[1]).wait_send()
            return carry

        lax.fori_loop(1, number, sent, 0)


def per_device(
    targets,
    points,
    tree_order,
    leaf_basis,
    transfer_local,
    coupling_local,
    transfer_top,
    coupling_top,
):
    spread = lax.axis_size("rhs")
    count = lax.axis_size("leaf")
    bits = count.bit_length() - 1
    group = 1 << (bits + 1) // 2
    planes = count // group
    leaves = leaf_basis.shape[0]
    columns, here = targets.shape
    nodes = group - 1 + planes - 1
    loads = 3 + 2 * (group.bit_length())
    most = max(group, planes)
    vmem = pl.BlockSpec(memory_space=pltpu.VMEM)
    any_space = pl.BlockSpec(memory_space=pl.ANY)
    out = jax.ShapeDtypeStruct((columns, here), f32)
    return pl.pallas_call(
        functools.partial(whole_kernel, (spread, group, planes, leaves)),
        out_shape=(out, out),
        in_specs=[vmem, vmem, vmem] + [any_space] * 5,
        out_specs=(vmem, vmem),
        scratch_shapes=[
            pltpu.VMEM(leaf_basis.shape, bf16),
            pltpu.VMEM(transfer_local.shape, bf16),
            pltpu.VMEM(coupling_local.shape, bf16),
            pltpu.VMEM((nodes, RANK, 2 * RANK), bf16),
            pltpu.VMEM((nodes, RANK, RANK), bf16),
            pltpu.VMEM((leaves * 8, LEAF), f32),
            pltpu.VMEM((leaves * 8, LEAF), bf16),
            pltpu.VMEM((leaves * 16, LEAF), bf16),
            pltpu.VMEM((leaves, LEAF, LEAF), bf16),
            pltpu.VMEM((leaves, LEAF, LEAF), bf16),
            pltpu.VMEM((leaves, LEAF, LEAF), bf16),
            pltpu.VMEM((leaves, ROWS, LEAF), f32),
            pltpu.VMEM((leaves, ROWS, LEAF), f32),
            pltpu.VMEM((leaves, ROWS, LEAF), f32),
            pltpu.VMEM((2, leaves, ROWS, LEAF), f32),
            pltpu.VMEM((2 * leaves * 8, LEAF), f32),
            pltpu.VMEM((2, leaves - 1, ROWS, RANK), f32),
            pltpu.VMEM((ROUNDS, most, ROWS, RANK), f32),
            pltpu.SemaphoreType.DMA((loads,)),
            pltpu.SemaphoreType.DMA((2, spread - 1)),
            pltpu.SemaphoreType.DMA((2, spread)),
            pltpu.SemaphoreType.DMA((ROUNDS, most - 1)),
            pltpu.SemaphoreType.DMA((ROUNDS, most)),
        ],
        compiler_params=pltpu.CompilerParams(
            collective_id=0, has_side_effects=True, vmem_limit_bytes=56 * 1024 * 1024
        ),
        name="ridge",
    )(
        targets,
        points,
        tree_order.reshape(-1, RANK),
        leaf_basis,
        transfer_local,
        coupling_local,
        transfer_top.transpose(0, 2, 1),
        coupling_top.transpose(0, 2, 1),
    )


def solution(mesh):
    placed = (
        P("rhs", "leaf"),
        P(None, "leaf"),
        P("leaf"),
        P("leaf", None, None),
        P("leaf", None, None),
        P("leaf", None, None),
        P(None, None, "rhs"),
        P(None, None, "rhs"),
    )
    return jax.shard_map(
        per_device,
        mesh=mesh,
        in_specs=placed,
        out_specs=(P("rhs", "leaf"), P("rhs", "leaf")),
        check_vma=False,
    )
```

```python
import functools

import jax
import jax.numpy as jnp
from jax import lax
from jax.experimental import pallas as pl
from jax.experimental.pallas import tpu as pltpu
from jax.sharding import PartitionSpec as P

LEAF = 256
RANK = 128
DIMS = 8
ROWS = 8
kernel_rate = 0.0625
ridge_term = 1.0

f32 = jnp.float32
bf16 = jnp.bfloat16
MESH = pl.DeviceIdType.MESH
ROUNDS = 8


def rounded(values):
    return values.astype(bf16).astype(f32)


def batched(left, right):
    return lax.dot_general(left, right, (((2,), (1,)), ((0,), (0,))), preferred_element_type=f32)


def batched_t(left, right):
    return lax.dot_general(left, right, (((2,), (2,)), ((0,), (0,))), preferred_element_type=f32)


def up_level(coeffs, matrices, multiply=batched):
    half = coeffs.shape[0] // 2
    paired = coeffs.reshape(half, 2, ROWS, RANK)
    joined = jnp.concatenate([paired[:, 0], paired[:, 1]], axis=-1).astype(bf16)
    return rounded(multiply(joined, matrices)), paired


def whole_kernel(
    sizes,
    tgt_ref,
    pts_ref,
    idx_ref,
    basis_hbm,
    transfer_hbm,
    coupling_hbm,
    ttop_hbm,
    ctop_hbm,
    sol_ref,
    res_ref,
    basis,
    transfer,
    coupling,
    top_t,
    top_c,
    lhs_t32,
    lhs_t,
    lhs_p,
    onehot,
    k_high,
    k_low,
    vec,
    dense,
    image,
    first,
    acc,
    links,
    slots,
    load_sem,
    x_send,
    x_recv,
    t_send,
    t_recv,
):
    spread, group, planes, leaves = sizes
    leaf = lax.axis_index("leaf")
    mine = lax.axis_index("rhs")
    inner = lax.rem(leaf, group)
    plane = leaf // group
    base = plane * group

    barrier = pltpu.get_barrier_semaphore()

    def greet_inner(j, carry):
        other = base + lax.rem(inner + j, group)
        pl.semaphore_signal(barrier, inc=1, device_id=(other, mine), device_id_type=MESH)
        return carry

    def greet_plane(j, carry):
        other = inner + group * lax.rem(plane + j, planes)
        pl.semaphore_signal(barrier, inc=1, device_id=(other, mine), device_id_type=MESH)
        return carry

    def greet_x(j, carry):
        other = lax.rem(mine + j, spread)
        pl.semaphore_signal(barrier, inc=1, device_id=(leaf, other), device_id_type=MESH)
        return carry

    lax.fori_loop(1, group, greet_inner, 0)
    lax.fori_loop(1, planes, greet_plane, 0)
    lax.fori_loop(1, spread, greet_x, 0)

    width = RANK // spread
    mine_rows = pl.ds(pl.multiple_of(mine * width, width), width)
    tops = []
    low_levels = group.bit_length() - 1
    high_levels = planes.bit_length() - 1
    count = group * planes
    place = 0
    first_node = 0
    for level in range(low_levels):
        here = group >> level + 1
        tops.append((first_node + plane * here, place, here))
        place += here
        first_node += count >> level + 1
    tops.append((first_node, place, planes - 1))
    place += planes - 1
    nodes = place
    top_loads = []
    for i, (source, target, number) in enumerate(tops):
        for hbm, top, k in ((ttop_hbm, top_t, 0), (ctop_hbm, top_c, 1)):
            copy = pltpu.make_async_copy(
                hbm.at[pl.ds(source, number)],
                top.at[pl.ds(target, number), mine_rows],
                load_sem.at[3 + 2 * i + k],
            )
            copy.start()
            top_loads.append(copy)
    load_basis = pltpu.make_async_copy(basis_hbm, basis, load_sem.at[0])
    load_transfer = pltpu.make_async_copy(transfer_hbm, transfer, load_sem.at[1])
    load_coupling = pltpu.make_async_copy(coupling_hbm, coupling, load_sem.at[2])
    load_basis.start()
    load_transfer.start()
    load_coupling.start()
    pl.semaphore_wait(barrier, group - 1 + planes - 1 + spread - 1)

    low_nodes = group - 1
    parts = (pl.ds(0, low_nodes), pl.ds(low_nodes, nodes - low_nodes))

    def x_copies(part, owner, j, other):
        own_rows = pl.ds(pl.multiple_of(owner * width, width), width)
        return [
            pltpu.make_async_remote_copy(
                src_ref=top.at[parts[part], own_rows],
                dst_ref=top.at[parts[part], own_rows],
                send_sem=x_send.at[2 * part + k, j - 1],
                recv_sem=x_recv.at[2 * part + k, owner],
                device_id=(leaf, other),
                device_id_type=MESH,
            )
            for k, top in enumerate((top_t, top_c))
        ]

    def far_first(number):
        return sorted(range(1, number), key=lambda j: (-min(j, number - j), j))

    for part in range(2):
        for copy in top_loads[: 2 * low_levels] if part == 0 else top_loads[2 * low_levels :]:
            copy.wait()
        for j in far_first(spread):
            for copy in x_copies(part, mine, j, lax.rem(mine + j, spread)):
                copy.start()

    def x_wait(part):
        for j in far_first(spread):
            other = lax.rem(mine + j, spread)
            for copy in x_copies(part, other, j, other):
                copy.wait_recv()

    def tile_copy(turn, slot, j, other):
        return pltpu.make_async_remote_copy(
            src_ref=slots.at[turn, slot],
            dst_ref=slots.at[turn, slot],
            send_sem=t_send.at[turn, j - 1],
            recv_sem=t_recv.at[turn, slot],
            device_id=(other, mine),
            device_id_type=MESH,
        )

    def partner(turn, j):
        if turn % 2 == 0:
            slot = lax.rem(inner + j, group)
            return slot, base + slot
        slot = lax.rem(plane + j, planes)
        return slot, inner + group * slot

    def exchange_start(turn, tile):
        me, number = (inner, group) if turn % 2 == 0 else (plane, planes)
        slots[turn, me] = tile
        for j in far_first(number):
            tile_copy(turn, me, j, partner(turn, j)[1]).start()

    def exchange_wait(turn):
        number = group if turn % 2 == 0 else planes
        for j in reversed(far_first(number)):
            slot, other = partner(turn, j)
            tile_copy(turn, slot, j, other).wait_recv()
        return slots[turn, :number]

    for h in range(leaves):
        piece = tgt_ref[:, h * LEAF : (h + 1) * LEAF]
        high = rounded(piece)
        lhs_t32[h * 8 : h * 8 + 4, :] = high
        lhs_t32[h * 8 + 4 : h * 8 + 8, :] = piece - high
        piece = pts_ref[:, h * LEAF : (h + 1) * LEAF]
        high = rounded(piece)
        lhs_p[h * 16 : (h + 1) * 16, :] = jnp.concatenate([high, piece - high], axis=0).astype(bf16)
    lhs_t[...] = lhs_t32[...].astype(bf16)

    def index_row(c):
        return jnp.concatenate(
            [idx_ref[pl.ds(2 * c, 1), :], idx_ref[pl.ds(2 * c + 1, 1), :]], axis=1
        )

    def gather_leaf(c, carry):
        order = index_row(c)
        low = lax.bitwise_and(order, LEAF - 1)
        high = lax.shift_right_logical(order, 8)
        hot = lax.broadcasted_iota(jnp.int32, (LEAF, LEAF), 0) == low
        hot = jnp.where(hot, 1.0, 0.0).astype(bf16)
        onehot[c] = hot
        rows_t = jnp.dot(lhs_t[...], hot, preferred_element_type=f32).reshape(leaves, 8, LEAF)
        rows_p = jnp.dot(lhs_p[...], hot, preferred_element_type=f32).reshape(leaves, 16, LEAF)
        here_t = lax.broadcasted_iota(jnp.int32, (leaves, 8, LEAF), 0) == high[None]
        here_p = lax.broadcasted_iota(jnp.int32, (leaves, 16, LEAF), 0) == high[None]
        both = jnp.sum(jnp.where(here_t, rows_t, 0.0), axis=0)
        spots = jnp.sum(jnp.where(here_p, rows_p, 0.0), axis=0)
        vec[c] = both + pltpu.roll(both, 4, 0)
        spot_high, spot_low = spots[:8], spots[8:]
        whole = spot_high + spot_low
        norm = jnp.sum(whole * whole, axis=0, keepdims=True) * -kernel_rate
        norm_a = rounded(norm)
        norm_b = rounded(norm - norm_a)
        norm_c = norm - norm_a - norm_b
        row = lax.broadcasted_iota(jnp.int32, (8, LEAF), 0)
        norms = jnp.where(row == 0, norm_a, jnp.where(row == 1, norm_b, norm_c))
        ones = jnp.ones((8, LEAF), f32)
        zeros = jnp.zeros((8, LEAF), f32)
        tail_left = jnp.where(row < 3, norms, jnp.where(row < 6, ones, zeros))
        norms_up = jnp.where(row == 3, norm_a, jnp.where(row == 4, norm_b, norm_c))
        tail_right = jnp.where(row < 3, ones, jnp.where(row < 6, norms_up, zeros))
        left = jnp.concatenate(
            [spot_high, spot_high, spot_low, spot_low, tail_left, zeros], axis=0
        ).astype(bf16)
        right_high = spot_high * (2 * kernel_rate)
        right_low = spot_low * (2 * kernel_rate)
        right = jnp.concatenate(
            [right_high, right_low, right_high, right_low, tail_right, zeros], axis=0
        ).astype(bf16)
        power = lax.dot_general(left, right, (((0,), (0,)), ((), ())), preferred_element_type=f32)
        values = jnp.exp(power)
        values_high = values.astype(bf16)
        k_high[c] = values_high
        k_low[c] = (values - values_high.astype(f32)).astype(bf16)
        return carry

    lax.fori_loop(0, leaves, gather_leaf, 0, unroll=4)

    row8 = lax.broadcasted_iota(jnp.int32, (ROWS, RANK), 0)
    upper = row8 < 4

    def swap(tile):
        return pltpu.roll(tile, 4, 0)

    def lane_partial(product):
        total = jnp.sum(product, axis=0)
        return total[:, :RANK] + total[:, RANK:]

    def full(tile):
        return jnp.broadcast_to(jnp.sum(tile, axis=1, keepdims=True), (ROWS, RANK))

    def wide_of(tile):
        return jnp.concatenate([tile, tile], axis=1)[None]

    def both_halves(tile):
        return jnp.where(upper, tile, swap(tile))

    def level_links(level, pairs, place):
        spot, depth = (plane, level - low_levels) if level >= low_levels else (inner, level)
        node = lax.shift_right_logical(spot, depth + 1)
        side = lax.bitwise_and(lax.shift_right_logical(spot, depth), 1)
        sibling = jnp.zeros((ROWS, RANK), f32)
        for k in range(pairs.shape[0]):
            chosen = lax.shift_right_logical(spot, depth) + 1 - 2 * side == k
            sibling = jnp.where(chosen, pairs[k], sibling)
        sibling = sibling.astype(bf16)
        link = top_c[place + node]
        to_left = jnp.dot(sibling, link, preferred_element_type=f32)
        to_right = lax.dot_general(
            sibling, link, (((1,), (1,)), ((), ())), preferred_element_type=f32
        )
        return jnp.where(side == 0, to_left, to_right), side, place + node

    def level_product(pairs, place):
        half = pairs.shape[0] // 2
        paired = pairs.reshape(half, 2, ROWS, RANK)
        toward = batched(paired[:, 1].astype(bf16), top_c[place : place + half])
        return jnp.sum(paired[:, 0] * toward, axis=0)

    def apply_matrix(turn, extra):
        value = vec[...]
        square = lane_partial(value * value)
        coeffs = rounded(batched(value.astype(bf16), basis[...]))
        saved = []
        offset = 0
        number = leaves
        while number > 1:
            half = number // 2
            coeffs, paired = up_level(coeffs, transfer[offset : offset + half])
            saved.append((paired, offset, half))
            offset += half
            number = half
        exchange_start(turn, jnp.where(upper, coeffs[0], square))

        high = rounded(value)
        sub_row = lax.broadcasted_iota(jnp.int32, value.shape, 1)
        stacked = jnp.where(sub_row < 4, high, value - high).astype(bf16)
        product = batched(stacked, k_high[...]) + batched(stacked, k_low[...])
        product = product + pltpu.roll(product, 4, 1) + ridge_term * value
        dense[...] = product
        inside = jnp.zeros((ROWS, RANK), f32)
        for paired, offset, half in saved:
            matrices = coupling[offset : offset + half]
            toward = batched_t(paired[:, 1].astype(bf16), matrices)
            links[0, offset : offset + half] = toward
            links[1, offset : offset + half] = batched(paired[:, 0].astype(bf16), matrices)
            inside = inside + jnp.sum(paired[:, 0] * toward, axis=0)
        inside = 2.0 * inside + lane_partial(value * product)
        exchange_start(turn + 2, jnp.where(upper, inside, extra))

        if turn == 0:
            x_wait(0)
        tiles = exchange_wait(turn)
        group_square = jnp.sum(tiles, axis=0)
        levels = [tiles]
        starts = [0]
        place = 0
        for level in range(low_levels):
            half = levels[-1].shape[0] // 2
            levels.append(up_level(levels[-1], top_t[place : place + half], batched_t)[0])
            place += half
            starts.append(place)
        exchange_start(turn + 1, jnp.where(upper, levels.pop()[0], group_square))

        owns = [level_links(level, levels[level], starts[level]) for level in range(low_levels)]
        inside = jnp.zeros((ROWS, RANK), f32)
        for level in range(low_levels):
            inside = inside + level_product(levels[level], starts[level])
        group_sums = jnp.sum(exchange_wait(turn + 2), axis=0)
        exchange_start(turn + 3, group_sums + jnp.where(upper, 2.0 * inside, 0.0))

        if turn == 0:
            x_wait(1)
        tiles = exchange_wait(turn + 1)
        total_square = jnp.sum(tiles, axis=0)
        levels.append(tiles)
        for level in range(high_levels - 1):
            half = levels[-1].shape[0] // 2
            levels.append(up_level(levels[-1], top_t[place : place + half], batched_t)[0])
            place += half
            starts.append(place)
        for level in range(low_levels, low_levels + high_levels):
            owns.append(level_links(level, levels[level], starts[level]))

        field = None
        for own, side, node in reversed(owns):
            if field is not None:
                half_lanes = pl.multiple_of(side * RANK, RANK)
                half = top_t[node, :, pl.ds(half_lanes, RANK)]
                own = own + jnp.dot(field.astype(bf16), half, preferred_element_type=f32)
            field = own
        field = both_halves(field)[None]

        for _, offset, half in reversed(saved):
            child = batched_t(field.astype(bf16), transfer[offset : offset + half])
            left = child[:, :, :RANK] + links[0, offset : offset + half]
            right = child[:, :, RANK:] + links[1, offset : offset + half]
            field = jnp.stack([left, right], axis=1).reshape(2 * half, ROWS, RANK)
        image[...] = dense[...] + batched_t(field.astype(bf16), basis[...])

        inside = jnp.zeros((ROWS, RANK), f32)
        for level in range(low_levels, low_levels + high_levels):
            inside = inside + level_product(levels[level], starts[level])
        sums = jnp.sum(exchange_wait(turn + 3), axis=0)
        sums = full(sums + jnp.where(upper, 2.0 * inside, 0.0))
        total_square = full(total_square)
        return (
            jnp.where(upper, swap(total_square), total_square),
            both_halves(sums),
            jnp.where(upper, swap(sums), sums),
        )

    load_basis.wait()
    load_transfer.wait()
    load_coupling.wait()

    rr_first, curve_first, _ = apply_matrix(0, jnp.zeros((ROWS, RANK), f32))
    step_size = rr_first / curve_first
    start = vec[...]
    product = image[...]
    first[0] = start
    first[1] = product
    residual = start - wide_of(step_size) * product
    vec[...] = residual

    rr_second, curve, cross = apply_matrix(4, lane_partial(residual * product))
    ratio = rr_second / rr_first
    last_size = rr_second / (curve + 2.0 * ratio * cross + ratio * ratio * curve_first)
    residual = vec[...]
    direction = residual + wide_of(ratio) * first[0]
    product = image[...] + wide_of(ratio) * first[1]
    solution = wide_of(step_size) * first[0] + wide_of(last_size) * direction
    residual = residual - wide_of(last_size) * product
    sub_row = lax.broadcasted_iota(jnp.int32, residual.shape, 1)
    vec[...] = jnp.where(sub_row < 4, solution, residual)

    acc[...] = jnp.zeros_like(acc)

    def scatter_leaf(c, carry):
        order = index_row(c)
        high = lax.shift_right_logical(order, 8)
        here = lax.broadcasted_iota(jnp.int32, (leaves, 8, LEAF), 0) == high[None]
        value = vec[c]
        value_high = rounded(value)
        value_low = value - value_high
        part_high = jnp.where(here, value_high[None], 0.0).reshape(leaves * 8, LEAF)
        part_low = jnp.where(here, value_low[None], 0.0).reshape(leaves * 8, LEAF)
        rows = jnp.concatenate([part_high, part_low], axis=0).astype(bf16)
        acc[...] += lax.dot_general(
            rows, onehot[c], (((1,), (1,)), ((), ())), preferred_element_type=f32
        )
        return carry

    lax.fori_loop(0, leaves, scatter_leaf, 0, unroll=4)
    for h in range(leaves):
        tile = acc[h * 8 : h * 8 + 8, :] + acc[leaves * 8 + h * 8 : leaves * 8 + h * 8 + 8, :]
        sol_ref[:, h * LEAF : (h + 1) * LEAF] = tile[:4]
        res_ref[:, h * LEAF : (h + 1) * LEAF] = tile[4:]

    for part in range(2):
        for j in far_first(spread):
            for copy in x_copies(part, mine, j, lax.rem(mine + j, spread)):
                copy.wait_send()
    for turn in range(ROUNDS):
        me, number = (inner, group) if turn % 2 == 0 else (plane, planes)
        for j in far_first(number):
            tile_copy(turn, me, j, partner(turn, j)[1]).wait_send()


def per_device(
    targets,
    points,
    tree_order,
    leaf_basis,
    transfer_local,
    coupling_local,
    transfer_top,
    coupling_top,
):
    spread = lax.axis_size("rhs")
    count = lax.axis_size("leaf")
    bits = count.bit_length() - 1
    group = 1 << (bits + 1) // 2
    planes = count // group
    leaves = leaf_basis.shape[0]
    columns, here = targets.shape
    nodes = group - 1 + planes - 1
    loads = 3 + 2 * (group.bit_length())
    most = max(group, planes)
    vmem = pl.BlockSpec(memory_space=pltpu.VMEM)
    any_space = pl.BlockSpec(memory_space=pl.ANY)
    out = jax.ShapeDtypeStruct((columns, here), f32)
    return pl.pallas_call(
        functools.partial(whole_kernel, (spread, group, planes, leaves)),
        out_shape=(out, out),
        in_specs=[vmem, vmem, vmem] + [any_space] * 5,
        out_specs=(vmem, vmem),
        scratch_shapes=[
            pltpu.VMEM(leaf_basis.shape, bf16),
            pltpu.VMEM(transfer_local.shape, bf16),
            pltpu.VMEM(coupling_local.shape, bf16),
            pltpu.VMEM((nodes, RANK, 2 * RANK), bf16),
            pltpu.VMEM((nodes, RANK, RANK), bf16),
            pltpu.VMEM((leaves * 8, LEAF), f32),
            pltpu.VMEM((leaves * 8, LEAF), bf16),
            pltpu.VMEM((leaves * 16, LEAF), bf16),
            pltpu.VMEM((leaves, LEAF, LEAF), bf16),
            pltpu.VMEM((leaves, LEAF, LEAF), bf16),
            pltpu.VMEM((leaves, LEAF, LEAF), bf16),
            pltpu.VMEM((leaves, ROWS, LEAF), f32),
            pltpu.VMEM((leaves, ROWS, LEAF), f32),
            pltpu.VMEM((leaves, ROWS, LEAF), f32),
            pltpu.VMEM((2, leaves, ROWS, LEAF), f32),
            pltpu.VMEM((2 * leaves * 8, LEAF), f32),
            pltpu.VMEM((2, leaves - 1, ROWS, RANK), f32),
            pltpu.VMEM((ROUNDS, most, ROWS, RANK), f32),
            pltpu.SemaphoreType.DMA((loads,)),
            pltpu.SemaphoreType.DMA((4, spread - 1)),
            pltpu.SemaphoreType.DMA((4, spread)),
            pltpu.SemaphoreType.DMA((ROUNDS, most - 1)),
            pltpu.SemaphoreType.DMA((ROUNDS, most)),
        ],
        compiler_params=pltpu.CompilerParams(
            collective_id=0, has_side_effects=True, vmem_limit_bytes=56 * 1024 * 1024
        ),
        name="ridge",
    )(
        targets,
        points,
        tree_order.reshape(-1, RANK),
        leaf_basis,
        transfer_local,
        coupling_local,
        transfer_top.transpose(0, 2, 1),
        coupling_top.transpose(0, 2, 1),
    )


def solution(mesh):
    placed = (
        P("rhs", "leaf"),
        P(None, "leaf"),
        P("leaf"),
        P("leaf", None, None),
        P("leaf", None, None),
        P("leaf", None, None),
        P(None, None, "rhs"),
        P(None, None, "rhs"),
    )
    return jax.shard_map(
        per_device,
        mesh=mesh,
        in_specs=placed,
        out_specs=(P("rhs", "leaf"), P("rhs", "leaf")),
        check_vma=False,
    )
```

```python
import functools

import jax
import jax.numpy as jnp
from jax import lax
from jax.experimental import pallas as pl
from jax.experimental.pallas import tpu as pltpu
from jax.sharding import PartitionSpec as P

LEAF = 256
RANK = 128
DIMS = 8
ROWS = 8
kernel_rate = 0.0625
ridge_term = 1.0

f32 = jnp.float32
bf16 = jnp.bfloat16
MESH = pl.DeviceIdType.MESH
ROUNDS = 8
UNROLL = 8


def rounded(values):
    return values.astype(bf16).astype(f32)


def batched(left, right):
    return lax.dot_general(left, right, (((2,), (1,)), ((0,), (0,))), preferred_element_type=f32)


def batched_t(left, right):
    return lax.dot_general(left, right, (((2,), (2,)), ((0,), (0,))), preferred_element_type=f32)


def up_level(coeffs, matrices, multiply=batched):
    half = coeffs.shape[0] // 2
    paired = coeffs.reshape(half, 2, ROWS, RANK)
    joined = jnp.concatenate([paired[:, 0], paired[:, 1]], axis=-1).astype(bf16)
    return rounded(multiply(joined, matrices)), paired


def whole_kernel(
    sizes,
    tgt_ref,
    pts_ref,
    idx_ref,
    basis_hbm,
    transfer_hbm,
    coupling_hbm,
    ttop_hbm,
    ctop_hbm,
    sol_ref,
    res_ref,
    basis,
    transfer,
    coupling,
    top_t,
    top_c,
    lhs_t32,
    lhs_t,
    lhs_p,
    onehot,
    k_high,
    k_low,
    vec,
    dense,
    image,
    first,
    acc,
    links,
    slots,
    load_sem,
    x_send,
    x_recv,
    h_send,
    h_recv,
    t_send,
    t_recv,
):
    spread, group, planes, leaves = sizes
    leaf = lax.axis_index("leaf")
    mine = lax.axis_index("rhs")
    inner = lax.rem(leaf, group)
    plane = leaf // group
    base = plane * group

    barrier = pltpu.get_barrier_semaphore()

    def greet_inner(j, carry):
        other = base + lax.rem(inner + j, group)
        pl.semaphore_signal(barrier, inc=1, device_id=(other, mine), device_id_type=MESH)
        return carry

    def greet_plane(j, carry):
        other = inner + group * lax.rem(plane + j, planes)
        pl.semaphore_signal(barrier, inc=1, device_id=(other, mine), device_id_type=MESH)
        return carry

    def greet_x(j, carry):
        other = lax.rem(mine + j, spread)
        pl.semaphore_signal(barrier, inc=1, device_id=(leaf, other), device_id_type=MESH)
        return carry

    lax.fori_loop(1, group, greet_inner, 0)
    lax.fori_loop(1, planes, greet_plane, 0)
    lax.fori_loop(1, spread, greet_x, 0)

    width = RANK // spread
    mine_rows = pl.ds(pl.multiple_of(mine * width, width), width)
    tops = []
    low_levels = group.bit_length() - 1
    high_levels = planes.bit_length() - 1
    count = group * planes
    place = 0
    first_node = 0
    for level in range(low_levels):
        here = group >> level + 1
        tops.append((first_node + plane * here, place, here))
        place += here
        first_node += count >> level + 1
    tops.append((first_node, place, planes - 1))
    place += planes - 1
    nodes = place
    top_loads = []
    for i, (source, target, number) in enumerate(tops):
        for hbm, top, k in ((ttop_hbm, top_t, 0), (ctop_hbm, top_c, 1)):
            copy = pltpu.make_async_copy(
                hbm.at[pl.ds(source, number)],
                top.at[pl.ds(target, number), mine_rows],
                load_sem.at[3 + 2 * i + k],
            )
            copy.start()
            top_loads.append(copy)
    load_basis = pltpu.make_async_copy(basis_hbm, basis, load_sem.at[0])
    load_transfer = pltpu.make_async_copy(transfer_hbm, transfer, load_sem.at[1])
    load_coupling = pltpu.make_async_copy(coupling_hbm, coupling, load_sem.at[2])
    load_basis.start()
    load_transfer.start()
    load_coupling.start()
    low_nodes = group - 1
    parts = (pl.ds(0, low_nodes), pl.ds(low_nodes, nodes - low_nodes))
    core = lax.rem(leaf, 2)
    pair = leaf + 1 - 2 * core
    half_width = width // 2

    def x_copies(part, owner, half, sems, slot, place):
        first_row = pl.multiple_of(owner * width + half * half_width, half_width)
        rows = pl.ds(first_row, half_width)
        send, recv = sems
        return [
            pltpu.make_async_remote_copy(
                src_ref=top.at[parts[part], rows],
                dst_ref=top.at[parts[part], rows],
                send_sem=send.at[2 * part + k, slot],
                recv_sem=recv.at[2 * part + k, owner],
                device_id=place,
                device_id_type=MESH,
            )
            for k, top in enumerate((top_t, top_c))
        ]

    def far_first(number):
        return sorted(range(1, number), key=lambda j: (-min(j, number - j), j))

    across, handed = (x_send, x_recv), (h_send, h_recv)

    def x_start():
        for part in range(2):
            for copy in top_loads[: 2 * low_levels] if part == 0 else top_loads[2 * low_levels :]:
                copy.wait()
            for j in far_first(spread):
                place = (leaf, lax.rem(mine + j, spread))
                for copy in x_copies(part, mine, core, across, j - 1, place):
                    copy.start()

    def x_hand_over(part):
        for j in reversed(far_first(spread)):
            other = lax.rem(mine + j, spread)
            for copy in x_copies(part, other, core, across, j - 1, (leaf, other)):
                copy.wait_recv()
            for copy in x_copies(part, other, core, handed, j - 1, (pair, mine)):
                copy.start()

    def x_wait(part):
        for j in reversed(far_first(spread)):
            other = lax.rem(mine + j, spread)
            for copy in x_copies(part, other, 1 - core, handed, j - 1, (pair, mine)):
                copy.wait_recv()

    pl.semaphore_wait(barrier, group - 1 + planes - 1 + spread - 1)
    x_start()

    def tile_copy(turn, slot, j, other):
        return pltpu.make_async_remote_copy(
            src_ref=slots.at[turn, slot],
            dst_ref=slots.at[turn, slot],
            send_sem=t_send.at[turn, j - 1],
            recv_sem=t_recv.at[turn, slot],
            device_id=(other, mine),
            device_id_type=MESH,
        )

    def partner(turn, j):
        if turn % 2 == 0:
            slot = lax.rem(inner + j, group)
            return slot, base + slot
        slot = lax.rem(plane + j, planes)
        return slot, inner + group * slot

    def exchange_start(turn, tile):
        me, number = (inner, group) if turn % 2 == 0 else (plane, planes)
        slots[turn, me] = tile
        for j in far_first(number):
            tile_copy(turn, me, j, partner(turn, j)[1]).start()

    def exchange_wait(turn):
        number = group if turn % 2 == 0 else planes
        for j in reversed(far_first(number)):
            slot, other = partner(turn, j)
            tile_copy(turn, slot, j, other).wait_recv()
        return slots[turn, :number]

    for h in range(leaves):
        piece = tgt_ref[:, h * LEAF : (h + 1) * LEAF]
        high = rounded(piece)
        lhs_t32[h * 8 : h * 8 + 4, :] = high
        lhs_t32[h * 8 + 4 : h * 8 + 8, :] = piece - high
        piece = pts_ref[:, h * LEAF : (h + 1) * LEAF]
        high = rounded(piece)
        lhs_p[h * 16 : (h + 1) * 16, :] = jnp.concatenate([high, piece - high], axis=0).astype(bf16)
    lhs_t[...] = lhs_t32[...].astype(bf16)

    def index_row(c):
        return jnp.concatenate(
            [idx_ref[pl.ds(2 * c, 1), :], idx_ref[pl.ds(2 * c + 1, 1), :]], axis=1
        )

    def gather_leaf(c, carry):
        order = index_row(c)
        low = lax.bitwise_and(order, LEAF - 1)
        high = lax.shift_right_logical(order, 8)
        hot = lax.broadcasted_iota(jnp.int32, (LEAF, LEAF), 0) == low
        hot = jnp.where(hot, 1.0, 0.0).astype(bf16)
        onehot[c] = hot
        rows_t = jnp.dot(lhs_t[...], hot, preferred_element_type=f32).reshape(leaves, 8, LEAF)
        rows_p = jnp.dot(lhs_p[...], hot, preferred_element_type=f32).reshape(leaves, 16, LEAF)
        here = lax.broadcasted_iota(jnp.int32, (leaves, 8, LEAF), 0) == high[None]
        both = jnp.sum(jnp.where(here, rows_t, 0.0), axis=0)
        spot_high = jnp.sum(jnp.where(here, rows_p[:, :8], 0.0), axis=0)
        spot_low = jnp.sum(jnp.where(here, rows_p[:, 8:], 0.0), axis=0)
        vec[c] = both + pltpu.roll(both, 4, 0)
        whole = spot_high + spot_low
        norm = jnp.sum(whole * whole, axis=0, keepdims=True) * -kernel_rate
        norm_a = rounded(norm)
        norm_b = rounded(norm - norm_a)
        norm_c = norm - norm_a - norm_b
        row = lax.broadcasted_iota(jnp.int32, (8, LEAF), 0)
        norms = jnp.where(row == 0, norm_a, jnp.where(row == 1, norm_b, norm_c))
        ones = jnp.ones((8, LEAF), f32)
        zeros = jnp.zeros((8, LEAF), f32)
        tail_left = jnp.where(row < 3, norms, jnp.where(row < 6, ones, zeros))
        norms_up = jnp.where(row == 3, norm_a, jnp.where(row == 4, norm_b, norm_c))
        tail_right = jnp.where(row < 3, ones, jnp.where(row < 6, norms_up, zeros))
        left = jnp.concatenate(
            [spot_high, spot_high, spot_low, spot_low, tail_left, zeros], axis=0
        ).astype(bf16)
        right_high = spot_high * (2 * kernel_rate)
        right_low = spot_low * (2 * kernel_rate)
        right = jnp.concatenate(
            [right_high, right_low, right_high, right_low, tail_right, zeros], axis=0
        ).astype(bf16)
        power = lax.dot_general(left, right, (((0,), (0,)), ((), ())), preferred_element_type=f32)
        values = jnp.exp(power)
        values_high = values.astype(bf16)
        k_high[c] = values_high
        k_low[c] = (values - values_high.astype(f32)).astype(bf16)
        return carry

    lax.fori_loop(0, leaves, gather_leaf, 0, unroll=min(UNROLL, leaves))

    row8 = lax.broadcasted_iota(jnp.int32, (ROWS, RANK), 0)
    upper = row8 < 4

    def swap(tile):
        return pltpu.roll(tile, 4, 0)

    def lane_partial(product):
        total = jnp.sum(product, axis=0)
        return total[:, :RANK] + total[:, RANK:]

    def full(tile):
        return jnp.broadcast_to(jnp.sum(tile, axis=1, keepdims=True), (ROWS, RANK))

    def wide_of(tile):
        return jnp.concatenate([tile, tile], axis=1)[None]

    def both_halves(tile):
        return jnp.where(upper, tile, swap(tile))

    def level_links(level, pairs, place):
        spot, depth = (plane, level - low_levels) if level >= low_levels else (inner, level)
        node = lax.shift_right_logical(spot, depth + 1)
        side = lax.bitwise_and(lax.shift_right_logical(spot, depth), 1)
        sibling = jnp.zeros((ROWS, RANK), f32)
        for k in range(pairs.shape[0]):
            chosen = lax.shift_right_logical(spot, depth) + 1 - 2 * side == k
            sibling = jnp.where(chosen, pairs[k], sibling)
        sibling = sibling.astype(bf16)
        link = top_c[place + node]
        to_left = jnp.dot(sibling, link, preferred_element_type=f32)
        to_right = lax.dot_general(
            sibling, link, (((1,), (1,)), ((), ())), preferred_element_type=f32
        )
        return jnp.where(side == 0, to_left, to_right), side, place + node

    def level_product(pairs, place):
        half = pairs.shape[0] // 2
        paired = pairs.reshape(half, 2, ROWS, RANK)
        toward = batched(paired[:, 1].astype(bf16), top_c[place : place + half])
        return jnp.sum(paired[:, 0] * toward, axis=0)

    def apply_matrix(turn, extra):
        value = vec[...]
        square = lane_partial(value * value)
        coeffs = rounded(batched(value.astype(bf16), basis[...]))
        saved = []
        offset = 0
        number = leaves
        while number > 1:
            half = number // 2
            coeffs, paired = up_level(coeffs, transfer[offset : offset + half])
            saved.append((paired, offset, half))
            offset += half
            number = half
        exchange_start(turn, jnp.where(upper, coeffs[0], square))

        high = rounded(value)
        sub_row = lax.broadcasted_iota(jnp.int32, value.shape, 1)
        stacked = jnp.where(sub_row < 4, high, value - high).astype(bf16)
        product = batched(stacked, k_high[...]) + batched(stacked, k_low[...])
        product = product + pltpu.roll(product, 4, 1) + ridge_term * value
        dense[...] = product
        inside = jnp.zeros((ROWS, RANK), f32)
        for paired, offset, half in saved:
            matrices = coupling[offset : offset + half]
            toward = batched_t(paired[:, 1].astype(bf16), matrices)
            links[0, offset : offset + half] = toward
            links[1, offset : offset + half] = batched(paired[:, 0].astype(bf16), matrices)
            inside = inside + jnp.sum(paired[:, 0] * toward, axis=0)
        inside = 2.0 * inside + lane_partial(value * product)
        exchange_start(turn + 2, jnp.where(upper, inside, extra))

        if turn == 0:
            x_hand_over(0)
        tiles = exchange_wait(turn)
        group_square = jnp.sum(tiles, axis=0)
        if turn == 0:
            x_wait(0)
        levels = [tiles]
        starts = [0]
        place = 0
        for level in range(low_levels):
            half = levels[-1].shape[0] // 2
            levels.append(up_level(levels[-1], top_t[place : place + half], batched_t)[0])
            place += half
            starts.append(place)
        exchange_start(turn + 1, jnp.where(upper, levels.pop()[0], group_square))

        owns = [level_links(level, levels[level], starts[level]) for level in range(low_levels)]
        inside = jnp.zeros((ROWS, RANK), f32)
        for level in range(low_levels):
            inside = inside + level_product(levels[level], starts[level])
        group_sums = jnp.sum(exchange_wait(turn + 2), axis=0)
        exchange_start(turn + 3, group_sums + jnp.where(upper, 2.0 * inside, 0.0))

        if turn == 0:
            x_hand_over(1)
        tiles = exchange_wait(turn + 1)
        total_square = jnp.sum(tiles, axis=0)
        if turn == 0:
            x_wait(1)
        levels.append(tiles)
        for level in range(high_levels - 1):
            half = levels[-1].shape[0] // 2
            levels.append(up_level(levels[-1], top_t[place : place + half], batched_t)[0])
            place += half
            starts.append(place)
        for level in range(low_levels, low_levels + high_levels):
            owns.append(level_links(level, levels[level], starts[level]))

        field = None
        for own, side, node in reversed(owns):
            if field is not None:
                half_lanes = pl.multiple_of(side * RANK, RANK)
                half = top_t[node, :, pl.ds(half_lanes, RANK)]
                own = own + jnp.dot(field.astype(bf16), half, preferred_element_type=f32)
            field = own
        field = both_halves(field)[None]

        for _, offset, half in reversed(saved):
            child = batched_t(field.astype(bf16), transfer[offset : offset + half])
            left = child[:, :, :RANK] + links[0, offset : offset + half]
            right = child[:, :, RANK:] + links[1, offset : offset + half]
            field = jnp.stack([left, right], axis=1).reshape(2 * half, ROWS, RANK)
        image[...] = dense[...] + batched_t(field.astype(bf16), basis[...])

        inside = jnp.zeros((ROWS, RANK), f32)
        for level in range(low_levels, low_levels + high_levels):
            inside = inside + level_product(levels[level], starts[level])
        sums = jnp.sum(exchange_wait(turn + 3), axis=0)
        sums = full(sums + jnp.where(upper, 2.0 * inside, 0.0))
        total_square = full(total_square)
        return (
            jnp.where(upper, swap(total_square), total_square),
            both_halves(sums),
            jnp.where(upper, swap(sums), sums),
        )

    load_basis.wait()
    load_transfer.wait()
    load_coupling.wait()

    rr_first, curve_first, _ = apply_matrix(0, jnp.zeros((ROWS, RANK), f32))
    step_size = rr_first / curve_first
    start = vec[...]
    product = image[...]
    first[0] = start
    first[1] = product
    residual = start - wide_of(step_size) * product
    vec[...] = residual

    rr_second, curve, cross = apply_matrix(4, lane_partial(residual * product))
    ratio = rr_second / rr_first
    last_size = rr_second / (curve + 2.0 * ratio * cross + ratio * ratio * curve_first)
    residual = vec[...]
    direction = residual + wide_of(ratio) * first[0]
    product = image[...] + wide_of(ratio) * first[1]
    solution = wide_of(step_size) * first[0] + wide_of(last_size) * direction
    residual = residual - wide_of(last_size) * product
    sub_row = lax.broadcasted_iota(jnp.int32, residual.shape, 1)
    vec[...] = jnp.where(sub_row < 4, solution, residual)

    acc[...] = jnp.zeros_like(acc)

    def scatter_leaf(c, carry):
        order = index_row(c)
        high = lax.shift_right_logical(order, 8)
        here = lax.broadcasted_iota(jnp.int32, (leaves, 8, LEAF), 0) == high[None]
        value = vec[c]
        value_high = rounded(value)
        value_low = value - value_high
        part_high = jnp.where(here, value_high[None], 0.0).reshape(leaves * 8, LEAF)
        part_low = jnp.where(here, value_low[None], 0.0).reshape(leaves * 8, LEAF)
        rows = jnp.concatenate([part_high, part_low], axis=0).astype(bf16)
        acc[...] += lax.dot_general(
            rows, onehot[c], (((1,), (1,)), ((), ())), preferred_element_type=f32
        )
        return carry

    lax.fori_loop(0, leaves, scatter_leaf, 0, unroll=min(UNROLL, leaves))
    for h in range(leaves):
        tile = acc[h * 8 : h * 8 + 8, :] + acc[leaves * 8 + h * 8 : leaves * 8 + h * 8 + 8, :]
        sol_ref[:, h * LEAF : (h + 1) * LEAF] = tile[:4]
        res_ref[:, h * LEAF : (h + 1) * LEAF] = tile[4:]

    for part in range(2):
        for j in far_first(spread):
            other = lax.rem(mine + j, spread)
            for copy in x_copies(part, mine, core, across, j - 1, (leaf, other)):
                copy.wait_send()
            for copy in x_copies(part, other, core, handed, j - 1, (pair, mine)):
                copy.wait_send()
    for turn in range(ROUNDS):
        me, number = (inner, group) if turn % 2 == 0 else (plane, planes)
        for j in far_first(number):
            tile_copy(turn, me, j, partner(turn, j)[1]).wait_send()


def hand_out(sol_in, res_in, sol_out, res_out, sem):
    copies = [
        pltpu.make_async_copy(sol_in, sol_out, sem.at[0]),
        pltpu.make_async_copy(res_in, res_out, sem.at[1]),
    ]
    for copy in copies:
        copy.start()
    for copy in copies:
        copy.wait()


def per_device(
    targets,
    points,
    tree_order,
    leaf_basis,
    transfer_local,
    coupling_local,
    transfer_top,
    coupling_top,
):
    spread = lax.axis_size("rhs")
    count = lax.axis_size("leaf")
    bits = count.bit_length() - 1
    group = 1 << (bits + 1) // 2
    planes = count // group
    leaves = leaf_basis.shape[0]
    columns, here = targets.shape
    nodes = group - 1 + planes - 1
    loads = 3 + 2 * (group.bit_length())
    most = max(group, planes)
    vmem = pl.BlockSpec(memory_space=pltpu.VMEM)
    any_space = pl.BlockSpec(memory_space=pl.ANY)
    hbm_space = pl.BlockSpec(memory_space=pltpu.HBM)
    out = jax.ShapeDtypeStruct((columns, here), f32)
    results = pl.pallas_call(
        functools.partial(whole_kernel, (spread, group, planes, leaves)),
        out_shape=(out, out),
        in_specs=[vmem, vmem, vmem] + [any_space] * 5,
        out_specs=(vmem, vmem),
        scratch_shapes=[
            pltpu.VMEM(leaf_basis.shape, bf16),
            pltpu.VMEM(transfer_local.shape, bf16),
            pltpu.VMEM(coupling_local.shape, bf16),
            pltpu.VMEM((nodes, RANK, 2 * RANK), bf16),
            pltpu.VMEM((nodes, RANK, RANK), bf16),
            pltpu.VMEM((leaves * 8, LEAF), f32),
            pltpu.VMEM((leaves * 8, LEAF), bf16),
            pltpu.VMEM((leaves * 16, LEAF), bf16),
            pltpu.VMEM((leaves, LEAF, LEAF), bf16),
            pltpu.VMEM((leaves, LEAF, LEAF), bf16),
            pltpu.VMEM((leaves, LEAF, LEAF), bf16),
            pltpu.VMEM((leaves, ROWS, LEAF), f32),
            pltpu.VMEM((leaves, ROWS, LEAF), f32),
            pltpu.VMEM((leaves, ROWS, LEAF), f32),
            pltpu.VMEM((2, leaves, ROWS, LEAF), f32),
            pltpu.VMEM((2 * leaves * 8, LEAF), f32),
            pltpu.VMEM((2, leaves - 1, ROWS, RANK), f32),
            pltpu.VMEM((ROUNDS, most, ROWS, RANK), f32),
            pltpu.SemaphoreType.DMA((loads,)),
            pltpu.SemaphoreType.DMA((4, spread - 1)),
            pltpu.SemaphoreType.DMA((4, spread)),
            pltpu.SemaphoreType.DMA((4, spread - 1)),
            pltpu.SemaphoreType.DMA((4, spread)),
            pltpu.SemaphoreType.DMA((ROUNDS, most - 1)),
            pltpu.SemaphoreType.DMA((ROUNDS, most)),
        ],
        compiler_params=pltpu.CompilerParams(
            collective_id=0, has_side_effects=True, vmem_limit_bytes=56 * 1024 * 1024
        ),
        name="ridge",
    )(
        targets,
        points,
        tree_order.reshape(-1, RANK),
        leaf_basis,
        transfer_local,
        coupling_local,
        transfer_top.transpose(0, 2, 1),
        coupling_top.transpose(0, 2, 1),
    )
    return pl.pallas_call(
        hand_out,
        out_shape=(out, out),
        in_specs=[vmem, vmem],
        out_specs=(hbm_space, hbm_space),
        scratch_shapes=[pltpu.SemaphoreType.DMA((2,))],
        name="hand_out",
    )(*results)


def solution(mesh):
    placed = (
        P("rhs", "leaf"),
        P(None, "leaf"),
        P("leaf"),
        P("leaf", None, None),
        P("leaf", None, None),
        P("leaf", None, None),
        P(None, None, "rhs"),
        P(None, None, "rhs"),
    )
    return jax.shard_map(
        per_device,
        mesh=mesh,
        in_specs=placed,
        out_specs=(P("rhs", "leaf"), P("rhs", "leaf")),
        check_vma=False,
    )
```

```python
import functools

import jax
import jax.numpy as jnp
from jax import lax
from jax.experimental import pallas as pl
from jax.experimental.pallas import tpu as pltpu
from jax.sharding import PartitionSpec as P

LEAF = 256
RANK = 128
DIMS = 8
ROWS = 8
kernel_rate = 0.0625
ridge_term = 1.0

f32 = jnp.float32
bf16 = jnp.bfloat16
MESH = pl.DeviceIdType.MESH
ROUNDS = 8
UNROLL = 8


def rounded(values):
    return values.astype(bf16).astype(f32)


def batched(left, right):
    return lax.dot_general(left, right, (((2,), (1,)), ((0,), (0,))), preferred_element_type=f32)


def batched_t(left, right):
    return lax.dot_general(left, right, (((2,), (2,)), ((0,), (0,))), preferred_element_type=f32)


def up_level(coeffs, matrices, multiply=batched):
    half = coeffs.shape[0] // 2
    paired = coeffs.reshape(half, 2, ROWS, RANK)
    joined = jnp.concatenate([paired[:, 0], paired[:, 1]], axis=-1).astype(bf16)
    return rounded(multiply(joined, matrices)), paired


def whole_kernel(
    sizes,
    tgt_ref,
    pts_ref,
    idx_ref,
    basis_hbm,
    transfer_hbm,
    coupling_hbm,
    ttop_hbm,
    ctop_hbm,
    sol_ref,
    res_ref,
    basis,
    transfer,
    coupling,
    top_t,
    top_c,
    lhs_t32,
    lhs_t,
    lhs_p,
    onehot,
    k_high,
    k_low,
    vec,
    dense,
    image,
    first,
    acc,
    links,
    slots,
    load_sem,
    x_send,
    x_recv,
    h_send,
    h_recv,
    t_send,
    t_recv,
):
    spread, group, planes, leaves = sizes
    leaf = lax.axis_index("leaf")
    mine = lax.axis_index("rhs")
    inner = lax.rem(leaf, group)
    plane = leaf // group
    base = plane * group

    barrier = pltpu.get_barrier_semaphore()

    def greet_inner(j, carry):
        other = base + lax.rem(inner + j, group)
        pl.semaphore_signal(barrier, inc=1, device_id=(other, mine), device_id_type=MESH)
        return carry

    def greet_plane(j, carry):
        other = inner + group * lax.rem(plane + j, planes)
        pl.semaphore_signal(barrier, inc=1, device_id=(other, mine), device_id_type=MESH)
        return carry

    def greet_x(j, carry):
        other = lax.rem(mine + j, spread)
        pl.semaphore_signal(barrier, inc=1, device_id=(leaf, other), device_id_type=MESH)
        return carry

    lax.fori_loop(1, group, greet_inner, 0)
    lax.fori_loop(1, planes, greet_plane, 0)
    lax.fori_loop(1, spread, greet_x, 0)

    width = RANK // spread
    mine_rows = pl.ds(pl.multiple_of(mine * width, width), width)
    tops = []
    low_levels = group.bit_length() - 1
    high_levels = planes.bit_length() - 1
    count = group * planes
    place = 0
    first_node = 0
    for level in range(low_levels):
        here = group >> level + 1
        tops.append((first_node + plane * here, place, here))
        place += here
        first_node += count >> level + 1
    tops.append((first_node, place, planes - 1))
    place += planes - 1
    nodes = place
    top_loads = []
    for i, (source, target, number) in enumerate(tops):
        for hbm, top, k in ((ttop_hbm, top_t, 0), (ctop_hbm, top_c, 1)):
            copy = pltpu.make_async_copy(
                hbm.at[pl.ds(source, number)],
                top.at[pl.ds(target, number), mine_rows],
                load_sem.at[3 + 2 * i + k],
            )
            copy.start()
            top_loads.append(copy)
    load_basis = pltpu.make_async_copy(basis_hbm, basis, load_sem.at[0])
    load_transfer = pltpu.make_async_copy(transfer_hbm, transfer, load_sem.at[1])
    load_coupling = pltpu.make_async_copy(coupling_hbm, coupling, load_sem.at[2])
    load_basis.start()
    load_transfer.start()
    load_coupling.start()
    low_nodes = group - 1
    parts = (pl.ds(0, low_nodes), pl.ds(low_nodes, nodes - low_nodes))
    core = lax.rem(leaf, 2)
    pair = leaf + 1 - 2 * core
    half_width = width // 2

    def x_copies(part, owner, half, sems, slot, place):
        first_row = pl.multiple_of(owner * width + half * half_width, half_width)
        rows = pl.ds(first_row, half_width)
        send, recv = sems
        return [
            pltpu.make_async_remote_copy(
                src_ref=top.at[parts[part], rows],
                dst_ref=top.at[parts[part], rows],
                send_sem=send.at[2 * part + k, slot],
                recv_sem=recv.at[2 * part + k, owner],
                device_id=place,
                device_id_type=MESH,
            )
            for k, top in enumerate((top_t, top_c))
        ]

    def far_first(number):
        return sorted(range(1, number), key=lambda j: (-min(j, number - j), j))

    across, handed = (x_send, x_recv), (h_send, h_recv)

    def x_start():
        for part in range(2):
            for copy in top_loads[: 2 * low_levels] if part == 0 else top_loads[2 * low_levels :]:
                copy.wait()
            for j in far_first(spread):
                place = (leaf, lax.rem(mine + j, spread))
                for copy in x_copies(part, mine, core, across, j - 1, place):
                    copy.start()

    def x_hand_over(part):
        for j in reversed(far_first(spread)):
            other = lax.rem(mine + j, spread)
            for copy in x_copies(part, other, core, across, j - 1, (leaf, other)):
                copy.wait_recv()
            for copy in x_copies(part, other, core, handed, j - 1, (pair, mine)):
                copy.start()

    def x_wait(part):
        for j in reversed(far_first(spread)):
            other = lax.rem(mine + j, spread)
            for copy in x_copies(part, other, 1 - core, handed, j - 1, (pair, mine)):
                copy.wait_recv()

    pl.semaphore_wait(barrier, group - 1 + planes - 1 + spread - 1)
    x_start()

    def tile_copy(turn, slot, j, other):
        return pltpu.make_async_remote_copy(
            src_ref=slots.at[turn, slot],
            dst_ref=slots.at[turn, slot],
            send_sem=t_send.at[turn, j - 1],
            recv_sem=t_recv.at[turn, slot],
            device_id=(other, mine),
            device_id_type=MESH,
        )

    def partner(turn, j):
        if turn % 2 == 0:
            slot = lax.rem(inner + j, group)
            return slot, base + slot
        slot = lax.rem(plane + j, planes)
        return slot, inner + group * slot

    def exchange_start(turn, tile):
        me, number = (inner, group) if turn % 2 == 0 else (plane, planes)
        slots[turn, me] = tile
        for j in far_first(number):
            tile_copy(turn, me, j, partner(turn, j)[1]).start()

    def exchange_wait(turn):
        number = group if turn % 2 == 0 else planes
        for j in reversed(far_first(number)):
            slot, other = partner(turn, j)
            tile_copy(turn, slot, j, other).wait_recv()
        return slots[turn, :number]

    for h in range(leaves):
        piece = tgt_ref[:, h * LEAF : (h + 1) * LEAF]
        high = rounded(piece)
        lhs_t32[h * 8 : h * 8 + 4, :] = high
        lhs_t32[h * 8 + 4 : h * 8 + 8, :] = piece - high
        piece = pts_ref[:, h * LEAF : (h + 1) * LEAF]
        high = rounded(piece)
        lhs_p[h * 16 : (h + 1) * 16, :] = jnp.concatenate([high, piece - high], axis=0).astype(bf16)
    lhs_t[...] = lhs_t32[...].astype(bf16)

    def index_row(c):
        return jnp.concatenate(
            [idx_ref[pl.ds(2 * c, 1), :], idx_ref[pl.ds(2 * c + 1, 1), :]], axis=1
        )

    def gather_leaf(c, carry):
        order = index_row(c)
        low = lax.bitwise_and(order, LEAF - 1)
        high = lax.shift_right_logical(order, 8)
        hot = lax.broadcasted_iota(jnp.int32, (LEAF, LEAF), 0) == low
        hot = jnp.where(hot, 1.0, 0.0).astype(bf16)
        onehot[c] = hot
        rows_t = jnp.dot(lhs_t[...], hot, preferred_element_type=f32).reshape(leaves, 8, LEAF)
        rows_p = jnp.dot(lhs_p[...], hot, preferred_element_type=f32).reshape(leaves, 16, LEAF)
        here = lax.broadcasted_iota(jnp.int32, (leaves, 8, LEAF), 0) == high[None]
        both = jnp.sum(jnp.where(here, rows_t, 0.0), axis=0)
        spot_high = jnp.sum(jnp.where(here, rows_p[:, :8], 0.0), axis=0)
        spot_low = jnp.sum(jnp.where(here, rows_p[:, 8:], 0.0), axis=0)
        vec[c] = both + pltpu.roll(both, 4, 0)
        whole = spot_high + spot_low
        norm = jnp.sum(whole * whole, axis=0, keepdims=True) * -kernel_rate
        norm_a = rounded(norm)
        norm_b = rounded(norm - norm_a)
        norm_c = norm - norm_a - norm_b
        row = lax.broadcasted_iota(jnp.int32, (8, LEAF), 0)
        norms = jnp.where(row == 0, norm_a, jnp.where(row == 1, norm_b, norm_c))
        ones = jnp.ones((8, LEAF), f32)
        zeros = jnp.zeros((8, LEAF), f32)
        tail_left = jnp.where(row < 3, norms, jnp.where(row < 6, ones, zeros))
        norms_up = jnp.where(row == 3, norm_a, jnp.where(row == 4, norm_b, norm_c))
        tail_right = jnp.where(row < 3, ones, jnp.where(row < 6, norms_up, zeros))
        left = jnp.concatenate(
            [spot_high, spot_high, spot_low, spot_low, tail_left, zeros], axis=0
        ).astype(bf16)
        right_high = spot_high * (2 * kernel_rate)
        right_low = spot_low * (2 * kernel_rate)
        right = jnp.concatenate(
            [right_high, right_low, right_high, right_low, tail_right, zeros], axis=0
        ).astype(bf16)
        power = lax.dot_general(left, right, (((0,), (0,)), ((), ())), preferred_element_type=f32)
        values = jnp.exp(power)
        values_high = values.astype(bf16)
        k_high[c] = values_high
        k_low[c] = (values - values_high.astype(f32)).astype(bf16)
        return carry

    lax.fori_loop(0, leaves, gather_leaf, 0, unroll=min(2 * UNROLL, leaves))

    row8 = lax.broadcasted_iota(jnp.int32, (ROWS, RANK), 0)
    upper = row8 < 4

    def swap(tile):
        return pltpu.roll(tile, 4, 0)

    def lane_partial(product):
        total = jnp.sum(product, axis=0)
        return total[:, :RANK] + total[:, RANK:]

    def full(tile):
        return jnp.broadcast_to(jnp.sum(tile, axis=1, keepdims=True), (ROWS, RANK))

    def wide_of(tile):
        return jnp.concatenate([tile, tile], axis=1)[None]

    def both_halves(tile):
        return jnp.where(upper, tile, swap(tile))

    def level_links(level, pairs, place):
        spot, depth = (plane, level - low_levels) if level >= low_levels else (inner, level)
        node = lax.shift_right_logical(spot, depth + 1)
        side = lax.bitwise_and(lax.shift_right_logical(spot, depth), 1)
        sibling = jnp.zeros((ROWS, RANK), f32)
        for k in range(pairs.shape[0]):
            chosen = lax.shift_right_logical(spot, depth) + 1 - 2 * side == k
            sibling = jnp.where(chosen, pairs[k], sibling)
        sibling = sibling.astype(bf16)
        link = top_c[place + node]
        to_left = jnp.dot(sibling, link, preferred_element_type=f32)
        to_right = lax.dot_general(
            sibling, link, (((1,), (1,)), ((), ())), preferred_element_type=f32
        )
        return jnp.where(side == 0, to_left, to_right), side, place + node

    def level_product(pairs, place):
        half = pairs.shape[0] // 2
        paired = pairs.reshape(half, 2, ROWS, RANK)
        toward = batched(paired[:, 1].astype(bf16), top_c[place : place + half])
        return jnp.sum(paired[:, 0] * toward, axis=0)

    def scatter(source, k):
        sub_row = lax.broadcasted_iota(jnp.int32, (ROWS, LEAF), 0)
        inner_steps = min(UNROLL, leaves)

        def step(i, carry):
            total = jnp.zeros((leaves * 8, LEAF), f32)
            for t in range(inner_steps):
                c = i * inner_steps + t
                high = lax.shift_right_logical(index_row(c), 8)
                here = lax.broadcasted_iota(jnp.int32, (leaves, 8, LEAF), 0) == high[None]
                value = source[c]
                value_high = rounded(value)
                pieces = jnp.where(sub_row < 4, value_high, value - value_high)
                rows = jnp.where(here, pieces[None], 0.0).reshape(leaves * 8, LEAF).astype(bf16)
                total = total + lax.dot_general(
                    rows, onehot[c], (((1,), (1,)), ((), ())), preferred_element_type=f32
                )
            acc[k] += total
            return carry

        acc[k] = jnp.zeros((leaves * 8, LEAF), f32)
        lax.fori_loop(0, leaves // inner_steps, step, 0)

    def apply_matrix(turn, extra):
        value = vec[...]
        square = lane_partial(value * value)
        coeffs = rounded(batched(value.astype(bf16), basis[...]))
        saved = []
        offset = 0
        number = leaves
        while number > 1:
            half = number // 2
            coeffs, paired = up_level(coeffs, transfer[offset : offset + half])
            saved.append((paired, offset, half))
            offset += half
            number = half
        exchange_start(turn, jnp.where(upper, coeffs[0], square))

        high = rounded(value)
        sub_row = lax.broadcasted_iota(jnp.int32, value.shape, 1)
        stacked = jnp.where(sub_row < 4, high, value - high).astype(bf16)
        product = batched(stacked, k_high[...]) + batched(stacked, k_low[...])
        product = product + pltpu.roll(product, 4, 1) + ridge_term * value
        dense[...] = product
        inside = jnp.zeros((ROWS, RANK), f32)
        for paired, offset, half in saved:
            matrices = coupling[offset : offset + half]
            toward = batched_t(paired[:, 1].astype(bf16), matrices)
            links[0, offset : offset + half] = toward
            links[1, offset : offset + half] = batched(paired[:, 0].astype(bf16), matrices)
            inside = inside + jnp.sum(paired[:, 0] * toward, axis=0)
        inside = 2.0 * inside + lane_partial(value * product)
        exchange_start(turn + 2, jnp.where(upper, inside, extra))

        if turn == 0:
            x_hand_over(0)
        tiles = exchange_wait(turn)
        group_square = jnp.sum(tiles, axis=0)
        if turn == 0:
            x_wait(0)
        levels = [tiles]
        starts = [0]
        place = 0
        for level in range(low_levels):
            half = levels[-1].shape[0] // 2
            levels.append(up_level(levels[-1], top_t[place : place + half], batched_t)[0])
            place += half
            starts.append(place)
        exchange_start(turn + 1, jnp.where(upper, levels.pop()[0], group_square))

        owns = [level_links(level, levels[level], starts[level]) for level in range(low_levels)]
        inside = jnp.zeros((ROWS, RANK), f32)
        for level in range(low_levels):
            inside = inside + level_product(levels[level], starts[level])
        if turn > 0:
            scatter(first, 0)
        group_sums = jnp.sum(exchange_wait(turn + 2), axis=0)
        exchange_start(turn + 3, group_sums + jnp.where(upper, 2.0 * inside, 0.0))

        if turn == 0:
            x_hand_over(1)
        tiles = exchange_wait(turn + 1)
        total_square = jnp.sum(tiles, axis=0)
        if turn == 0:
            x_wait(1)
        levels.append(tiles)
        for level in range(high_levels - 1):
            half = levels[-1].shape[0] // 2
            levels.append(up_level(levels[-1], top_t[place : place + half], batched_t)[0])
            place += half
            starts.append(place)
        for level in range(low_levels, low_levels + high_levels):
            owns.append(level_links(level, levels[level], starts[level]))

        field = None
        for own, side, node in reversed(owns):
            if field is not None:
                half_lanes = pl.multiple_of(side * RANK, RANK)
                half = top_t[node, :, pl.ds(half_lanes, RANK)]
                own = own + jnp.dot(field.astype(bf16), half, preferred_element_type=f32)
            field = own
        field = both_halves(field)[None]

        for _, offset, half in reversed(saved):
            child = batched_t(field.astype(bf16), transfer[offset : offset + half])
            left = child[:, :, :RANK] + links[0, offset : offset + half]
            right = child[:, :, RANK:] + links[1, offset : offset + half]
            field = jnp.stack([left, right], axis=1).reshape(2 * half, ROWS, RANK)
        image[...] = dense[...] + batched_t(field.astype(bf16), basis[...])
        if turn > 0:
            scatter(image, 1)

        inside = jnp.zeros((ROWS, RANK), f32)
        for level in range(low_levels, low_levels + high_levels):
            inside = inside + level_product(levels[level], starts[level])
        sums = jnp.sum(exchange_wait(turn + 3), axis=0)
        sums = full(sums + jnp.where(upper, 2.0 * inside, 0.0))
        total_square = full(total_square)
        return (
            jnp.where(upper, swap(total_square), total_square),
            both_halves(sums),
            jnp.where(upper, swap(sums), sums),
        )

    load_basis.wait()
    load_transfer.wait()
    load_coupling.wait()

    rr_first, curve_first, _ = apply_matrix(0, jnp.zeros((ROWS, RANK), f32))
    step_size = rr_first / curve_first
    start = vec[...]
    product = image[...]
    first[...] = product
    residual = start - wide_of(step_size) * product
    vec[...] = residual

    rr_second, curve, cross = apply_matrix(4, lane_partial(residual * product))
    ratio = rr_second / rr_first
    last_size = rr_second / (curve + 2.0 * ratio * cross + ratio * ratio * curve_first)
    step_size, ratio, last_size = (
        jnp.concatenate([tile, tile], axis=1)[:4] for tile in (step_size, ratio, last_size)
    )

    for h in range(leaves):
        tile = acc[0, h * 8 : h * 8 + 8, :]
        image_first = (tile + swap(tile))[:4]
        tile = acc[1, h * 8 : h * 8 + 8, :]
        image_second = (tile + swap(tile))[:4]
        start = tgt_ref[:, h * LEAF : (h + 1) * LEAF]
        residual = start - step_size * image_first
        direction = residual + ratio * start
        sol_ref[:, h * LEAF : (h + 1) * LEAF] = step_size * start + last_size * direction
        product = image_second + ratio * image_first
        res_ref[:, h * LEAF : (h + 1) * LEAF] = residual - last_size * product

    for part in range(2):
        for j in far_first(spread):
            other = lax.rem(mine + j, spread)
            for copy in x_copies(part, mine, core, across, j - 1, (leaf, other)):
                copy.wait_send()
            for copy in x_copies(part, other, core, handed, j - 1, (pair, mine)):
                copy.wait_send()
    for turn in range(ROUNDS):
        me, number = (inner, group) if turn % 2 == 0 else (plane, planes)
        for j in far_first(number):
            tile_copy(turn, me, j, partner(turn, j)[1]).wait_send()


def hand_out(sol_in, res_in, sol_out, res_out, sem):
    copies = [
        pltpu.make_async_copy(sol_in, sol_out, sem.at[0]),
        pltpu.make_async_copy(res_in, res_out, sem.at[1]),
    ]
    for copy in copies:
        copy.start()
    for copy in copies:
        copy.wait()


def per_device(
    targets,
    points,
    tree_order,
    leaf_basis,
    transfer_local,
    coupling_local,
    transfer_top,
    coupling_top,
):
    spread = lax.axis_size("rhs")
    count = lax.axis_size("leaf")
    bits = count.bit_length() - 1
    group = 1 << (bits + 1) // 2
    planes = count // group
    leaves = leaf_basis.shape[0]
    columns, here = targets.shape
    nodes = group - 1 + planes - 1
    loads = 3 + 2 * (group.bit_length())
    most = max(group, planes)
    vmem = pl.BlockSpec(memory_space=pltpu.VMEM)
    any_space = pl.BlockSpec(memory_space=pl.ANY)
    hbm_space = pl.BlockSpec(memory_space=pltpu.HBM)
    out = jax.ShapeDtypeStruct((columns, here), f32)
    results = pl.pallas_call(
        functools.partial(whole_kernel, (spread, group, planes, leaves)),
        out_shape=(out, out),
        in_specs=[vmem, vmem, vmem] + [any_space] * 5,
        out_specs=(vmem, vmem),
        scratch_shapes=[
            pltpu.VMEM(leaf_basis.shape, bf16),
            pltpu.VMEM(transfer_local.shape, bf16),
            pltpu.VMEM(coupling_local.shape, bf16),
            pltpu.VMEM((nodes, RANK, 2 * RANK), bf16),
            pltpu.VMEM((nodes, RANK, RANK), bf16),
            pltpu.VMEM((leaves * 8, LEAF), f32),
            pltpu.VMEM((leaves * 8, LEAF), bf16),
            pltpu.VMEM((leaves * 16, LEAF), bf16),
            pltpu.VMEM((leaves, LEAF, LEAF), bf16),
            pltpu.VMEM((leaves, LEAF, LEAF), bf16),
            pltpu.VMEM((leaves, LEAF, LEAF), bf16),
            pltpu.VMEM((leaves, ROWS, LEAF), f32),
            pltpu.VMEM((leaves, ROWS, LEAF), f32),
            pltpu.VMEM((leaves, ROWS, LEAF), f32),
            pltpu.VMEM((leaves, ROWS, LEAF), f32),
            pltpu.VMEM((2, leaves * 8, LEAF), f32),
            pltpu.VMEM((2, leaves - 1, ROWS, RANK), f32),
            pltpu.VMEM((ROUNDS, most, ROWS, RANK), f32),
            pltpu.SemaphoreType.DMA((loads,)),
            pltpu.SemaphoreType.DMA((4, spread - 1)),
            pltpu.SemaphoreType.DMA((4, spread)),
            pltpu.SemaphoreType.DMA((4, spread - 1)),
            pltpu.SemaphoreType.DMA((4, spread)),
            pltpu.SemaphoreType.DMA((ROUNDS, most - 1)),
            pltpu.SemaphoreType.DMA((ROUNDS, most)),
        ],
        compiler_params=pltpu.CompilerParams(
            collective_id=0, has_side_effects=True, vmem_limit_bytes=56 * 1024 * 1024
        ),
        name="ridge",
    )(
        targets,
        points,
        tree_order.reshape(-1, RANK),
        leaf_basis,
        transfer_local,
        coupling_local,
        transfer_top.transpose(0, 2, 1),
        coupling_top.transpose(0, 2, 1),
    )
    return pl.pallas_call(
        hand_out,
        out_shape=(out, out),
        in_specs=[vmem, vmem],
        out_specs=(hbm_space, hbm_space),
        scratch_shapes=[pltpu.SemaphoreType.DMA((2,))],
        name="hand_out",
    )(*results)


def solution(mesh):
    placed = (
        P("rhs", "leaf"),
        P(None, "leaf"),
        P("leaf"),
        P("leaf", None, None),
        P("leaf", None, None),
        P("leaf", None, None),
        P(None, None, "rhs"),
        P(None, None, "rhs"),
    )
    return jax.shard_map(
        per_device,
        mesh=mesh,
        in_specs=placed,
        out_specs=(P("rhs", "leaf"), P("rhs", "leaf")),
        check_vma=False,
    )
```

```python
import functools

import jax
import jax.numpy as jnp
from jax import lax
from jax.experimental import pallas as pl
from jax.experimental.pallas import tpu as pltpu
from jax.sharding import PartitionSpec as P

LEAF = 256
RANK = 128
DIMS = 8
ROWS = 8
kernel_rate = 0.0625
ridge_term = 1.0

f32 = jnp.float32
bf16 = jnp.bfloat16
MESH = pl.DeviceIdType.MESH
ROUNDS = 8
UNROLL = 8


def rounded(values):
    return values.astype(bf16).astype(f32)


def batched(left, right):
    return lax.dot_general(left, right, (((2,), (1,)), ((0,), (0,))), preferred_element_type=f32)


def batched_t(left, right):
    return lax.dot_general(left, right, (((2,), (2,)), ((0,), (0,))), preferred_element_type=f32)


def up_level(coeffs, matrices, multiply=batched):
    half = coeffs.shape[0] // 2
    paired = coeffs.reshape(half, 2, ROWS, RANK)
    joined = jnp.concatenate([paired[:, 0], paired[:, 1]], axis=-1).astype(bf16)
    return rounded(multiply(joined, matrices)), paired


def whole_kernel(
    sizes,
    tgt_ref,
    pts_ref,
    idx_ref,
    basis_hbm,
    transfer_hbm,
    coupling_hbm,
    ttop_hbm,
    ctop_hbm,
    sol_ref,
    res_ref,
    basis,
    transfer,
    coupling,
    top_t,
    top_c,
    lhs_t32,
    lhs_t,
    lhs_p,
    onehot,
    k_high,
    k_low,
    vec,
    dense,
    image,
    first,
    acc,
    links,
    slots,
    load_sem,
    x_send,
    x_recv,
    h_send,
    h_recv,
    t_send,
    t_recv,
    basis_t,
    transfer_t,
):
    spread, group, planes, leaves = sizes
    leaf = lax.axis_index("leaf")
    mine = lax.axis_index("rhs")
    inner = lax.rem(leaf, group)
    plane = leaf // group
    base = plane * group

    barrier = pltpu.get_barrier_semaphore()

    def greet_inner(j, carry):
        other = base + lax.rem(inner + j, group)
        pl.semaphore_signal(barrier, inc=1, device_id=(other, mine), device_id_type=MESH)
        return carry

    def greet_plane(j, carry):
        other = inner + group * lax.rem(plane + j, planes)
        pl.semaphore_signal(barrier, inc=1, device_id=(other, mine), device_id_type=MESH)
        return carry

    def greet_x(j, carry):
        other = lax.rem(mine + j, spread)
        pl.semaphore_signal(barrier, inc=1, device_id=(leaf, other), device_id_type=MESH)
        return carry

    width = RANK // spread
    mine_rows = pl.ds(pl.multiple_of(mine * width, width), width)
    tops = []
    low_levels = group.bit_length() - 1
    high_levels = planes.bit_length() - 1
    count = group * planes
    place = 0
    first_node = 0
    for level in range(low_levels):
        here = group >> level + 1
        tops.append((first_node + plane * here, place, here))
        place += here
        first_node += count >> level + 1
    tops.append((first_node, place, planes - 1))
    place += planes - 1
    nodes = place
    top_loads = []
    for i, (source, target, number) in enumerate(tops):
        for hbm, top, k in ((ttop_hbm, top_t, 0), (ctop_hbm, top_c, 1)):
            copy = pltpu.make_async_copy(
                hbm.at[pl.ds(source, number)],
                top.at[pl.ds(target, number), mine_rows],
                load_sem.at[3 + 2 * i + k],
            )
            copy.start()
            top_loads.append(copy)
    load_basis = pltpu.make_async_copy(basis_hbm, basis, load_sem.at[0])
    load_transfer = pltpu.make_async_copy(transfer_hbm, transfer, load_sem.at[1])
    load_coupling = pltpu.make_async_copy(coupling_hbm, coupling, load_sem.at[2])
    load_basis.start()
    load_transfer.start()
    load_coupling.start()

    lax.fori_loop(1, group, greet_inner, 0)
    lax.fori_loop(1, planes, greet_plane, 0)
    lax.fori_loop(1, spread, greet_x, 0)

    for h in range(leaves):
        piece = tgt_ref[:, h * LEAF : (h + 1) * LEAF]
        high = rounded(piece)
        lhs_t32[h * 8 : h * 8 + 4, :] = high
        lhs_t32[h * 8 + 4 : h * 8 + 8, :] = piece - high
        piece = pts_ref[:, h * LEAF : (h + 1) * LEAF]
        high = rounded(piece)
        lhs_p[h * 16 : (h + 1) * 16, :] = jnp.concatenate([high, piece - high], axis=0).astype(bf16)
    lhs_t[...] = lhs_t32[...].astype(bf16)

    low_nodes = group - 1
    parts = (pl.ds(0, low_nodes), pl.ds(low_nodes, nodes - low_nodes))
    core = lax.rem(leaf, 2)
    pair = leaf + 1 - 2 * core
    half_width = width // 2

    def x_copies(part, owner, half, sems, slot, place):
        first_row = pl.multiple_of(owner * width + half * half_width, half_width)
        rows = pl.ds(first_row, half_width)
        send, recv = sems
        return [
            pltpu.make_async_remote_copy(
                src_ref=top.at[parts[part], rows],
                dst_ref=top.at[parts[part], rows],
                send_sem=send.at[2 * part + k, slot],
                recv_sem=recv.at[2 * part + k, owner],
                device_id=place,
                device_id_type=MESH,
            )
            for k, top in enumerate((top_t, top_c))
        ]

    def far_first(number):
        return sorted(range(1, number), key=lambda j: (-min(j, number - j), j))

    across, handed = (x_send, x_recv), (h_send, h_recv)

    def x_start():
        for part in range(2):
            for copy in top_loads[: 2 * low_levels] if part == 0 else top_loads[2 * low_levels :]:
                copy.wait()
            for j in far_first(spread):
                place = (leaf, lax.rem(mine + j, spread))
                for copy in x_copies(part, mine, core, across, j - 1, place):
                    copy.start()

    def x_hand_over(part):
        for j in reversed(far_first(spread)):
            other = lax.rem(mine + j, spread)
            for copy in x_copies(part, other, core, across, j - 1, (leaf, other)):
                copy.wait_recv()
            for copy in x_copies(part, other, core, handed, j - 1, (pair, mine)):
                copy.start()

    def x_wait(part):
        for j in reversed(far_first(spread)):
            other = lax.rem(mine + j, spread)
            for copy in x_copies(part, other, 1 - core, handed, j - 1, (pair, mine)):
                copy.wait_recv()

    pl.semaphore_wait(barrier, group - 1 + planes - 1 + spread - 1)
    x_start()

    def tile_copy(turn, slot, j, other):
        return pltpu.make_async_remote_copy(
            src_ref=slots.at[turn, slot],
            dst_ref=slots.at[turn, slot],
            send_sem=t_send.at[turn, j - 1],
            recv_sem=t_recv.at[turn, slot],
            device_id=(other, mine),
            device_id_type=MESH,
        )

    def partner(turn, j):
        if turn % 2 == 0:
            slot = lax.rem(inner + j, group)
            return slot, base + slot
        slot = lax.rem(plane + j, planes)
        return slot, inner + group * slot

    def exchange_start(turn, tile):
        me, number = (inner, group) if turn % 2 == 0 else (plane, planes)
        slots[turn, me] = tile
        for j in far_first(number):
            tile_copy(turn, me, j, partner(turn, j)[1]).start()

    def exchange_wait(turn):
        number = group if turn % 2 == 0 else planes
        for j in reversed(far_first(number)):
            slot, other = partner(turn, j)
            tile_copy(turn, slot, j, other).wait_recv()
        return slots[turn, :number]

    def index_row(c):
        return jnp.concatenate(
            [idx_ref[pl.ds(2 * c, 1), :], idx_ref[pl.ds(2 * c + 1, 1), :]], axis=1
        )

    def gather_leaf(c, carry):
        order = index_row(c)
        low = lax.bitwise_and(order, LEAF - 1)
        high = lax.shift_right_logical(order, 8)
        hot = lax.broadcasted_iota(jnp.int32, (LEAF, LEAF), 0) == low
        hot = jnp.where(hot, 1.0, 0.0).astype(bf16)
        onehot[c] = hot
        rows_t = jnp.dot(lhs_t[...], hot, preferred_element_type=f32).reshape(leaves, 8, LEAF)
        rows_p = jnp.dot(lhs_p[...], hot, preferred_element_type=f32).reshape(leaves, 16, LEAF)
        here = lax.broadcasted_iota(jnp.int32, (leaves, 8, LEAF), 0) == high[None]
        both = jnp.sum(jnp.where(here, rows_t, 0.0), axis=0)
        spot_high = jnp.sum(jnp.where(here, rows_p[:, :8], 0.0), axis=0)
        spot_low = jnp.sum(jnp.where(here, rows_p[:, 8:], 0.0), axis=0)
        vec[c] = both + pltpu.roll(both, 4, 0)
        whole = spot_high + spot_low
        norm = jnp.sum(whole * whole, axis=0, keepdims=True) * -kernel_rate
        norm_a = rounded(norm)
        norm_b = rounded(norm - norm_a)
        norm_c = norm - norm_a - norm_b
        row = lax.broadcasted_iota(jnp.int32, (8, LEAF), 0)
        norms = jnp.where(row == 0, norm_a, jnp.where(row == 1, norm_b, norm_c))
        ones = jnp.ones((8, LEAF), f32)
        zeros = jnp.zeros((8, LEAF), f32)
        tail_left = jnp.where(row < 3, norms, jnp.where(row < 6, ones, zeros))
        norms_up = jnp.where(row == 3, norm_a, jnp.where(row == 4, norm_b, norm_c))
        tail_right = jnp.where(row < 3, ones, jnp.where(row < 6, norms_up, zeros))
        left = jnp.concatenate(
            [spot_high, spot_high, spot_low, spot_low, tail_left, zeros], axis=0
        ).astype(bf16)
        right_high = spot_high * (2 * kernel_rate)
        right_low = spot_low * (2 * kernel_rate)
        right = jnp.concatenate(
            [right_high, right_low, right_high, right_low, tail_right, zeros], axis=0
        ).astype(bf16)
        power = lax.dot_general(left, right, (((0,), (0,)), ((), ())), preferred_element_type=f32)
        values = jnp.exp(power)
        values_high = values.astype(bf16)
        k_high[c] = values_high
        k_low[c] = (values - values_high.astype(f32)).astype(bf16)
        return carry

    lax.fori_loop(0, leaves, gather_leaf, 0, unroll=min(2 * UNROLL, leaves))

    row8 = lax.broadcasted_iota(jnp.int32, (ROWS, RANK), 0)
    upper = row8 < 4

    def swap(tile):
        return pltpu.roll(tile, 4, 0)

    def lane_partial(product):
        total = jnp.sum(product, axis=0)
        return total[:, :RANK] + total[:, RANK:]

    def full(tile):
        return jnp.broadcast_to(jnp.sum(tile, axis=1, keepdims=True), (ROWS, RANK))

    def wide_of(tile):
        return jnp.concatenate([tile, tile], axis=1)[None]

    def both_halves(tile):
        return jnp.where(upper, tile, swap(tile))

    def level_links(level, pairs, place):
        spot, depth = (plane, level - low_levels) if level >= low_levels else (inner, level)
        node = lax.shift_right_logical(spot, depth + 1)
        side = lax.bitwise_and(lax.shift_right_logical(spot, depth), 1)
        sibling = jnp.zeros((ROWS, RANK), f32)
        for k in range(pairs.shape[0]):
            chosen = lax.shift_right_logical(spot, depth) + 1 - 2 * side == k
            sibling = jnp.where(chosen, pairs[k], sibling)
        sibling = sibling.astype(bf16)
        link = top_c[place + node]
        to_left = jnp.dot(sibling, link, preferred_element_type=f32)
        to_right = lax.dot_general(
            sibling, link, (((1,), (1,)), ((), ())), preferred_element_type=f32
        )
        return jnp.where(side == 0, to_left, to_right), side, place + node

    def level_product(pairs, place):
        half = pairs.shape[0] // 2
        paired = pairs.reshape(half, 2, ROWS, RANK)
        toward = batched(paired[:, 1].astype(bf16), top_c[place : place + half])
        return jnp.sum(paired[:, 0] * toward, axis=0)

    def scatter(source, k):
        sub_row = lax.broadcasted_iota(jnp.int32, (ROWS, LEAF), 0)
        inner_steps = min(2 * UNROLL, leaves)

        def step(i, carry):
            total = jnp.zeros((leaves * 8, LEAF), f32)
            for t in range(inner_steps):
                c = i * inner_steps + t
                high = lax.shift_right_logical(index_row(c), 8)
                here = lax.broadcasted_iota(jnp.int32, (leaves, 8, LEAF), 0) == high[None]
                value = source[c]
                value_high = rounded(value)
                pieces = jnp.where(sub_row < 4, value_high, value - value_high)
                rows = jnp.where(here, pieces[None], 0.0).reshape(leaves * 8, LEAF).astype(bf16)
                total = total + lax.dot_general(
                    rows, onehot[c], (((1,), (1,)), ((), ())), preferred_element_type=f32
                )
            acc[k] += total
            return carry

        acc[k] = jnp.zeros((leaves * 8, LEAF), f32)
        lax.fori_loop(0, leaves // inner_steps, step, 0)

    def apply_matrix(turn, extra):
        value = vec[...]
        square = lane_partial(value * value)
        coeffs = rounded(batched(value.astype(bf16), basis[...]))
        saved = []
        offset = 0
        number = leaves
        while number > 1:
            half = number // 2
            coeffs, paired = up_level(coeffs, transfer[offset : offset + half])
            saved.append((paired, offset, half))
            offset += half
            number = half
        exchange_start(turn, jnp.where(upper, coeffs[0], square))

        high = rounded(value)
        sub_row = lax.broadcasted_iota(jnp.int32, value.shape, 1)
        stacked = jnp.where(sub_row < 4, high, value - high).astype(bf16)
        product = batched(stacked, k_high[...]) + batched(stacked, k_low[...])
        product = product + pltpu.roll(product, 4, 1) + ridge_term * value
        dense[...] = product
        inside = jnp.zeros((ROWS, RANK), f32)
        for paired, offset, half in saved:
            matrices = coupling[offset : offset + half]
            toward = batched_t(paired[:, 1].astype(bf16), matrices)
            links[0, offset : offset + half] = toward
            links[1, offset : offset + half] = batched(paired[:, 0].astype(bf16), matrices)
            inside = inside + jnp.sum(paired[:, 0] * toward, axis=0)
        inside = 2.0 * inside + lane_partial(value * product)
        exchange_start(turn + 2, jnp.where(upper, inside, extra))

        if turn == 0:
            x_hand_over(0)
        tiles = exchange_wait(turn)
        group_square = jnp.sum(tiles, axis=0)
        if turn == 0:
            x_wait(0)
        levels = [tiles]
        starts = [0]
        place = 0
        for level in range(low_levels):
            half = levels[-1].shape[0] // 2
            levels.append(up_level(levels[-1], top_t[place : place + half], batched_t)[0])
            place += half
            starts.append(place)
        exchange_start(turn + 1, jnp.where(upper, levels.pop()[0], group_square))

        owns = [level_links(level, levels[level], starts[level]) for level in range(low_levels)]
        inside = jnp.zeros((ROWS, RANK), f32)
        for level in range(low_levels):
            inside = inside + level_product(levels[level], starts[level])
        if turn > 0:
            scatter(first, 0)
        group_sums = jnp.sum(exchange_wait(turn + 2), axis=0)
        exchange_start(turn + 3, group_sums + jnp.where(upper, 2.0 * inside, 0.0))

        if turn == 0:
            def turn_round(c, carry):
                basis_t[c] = basis[c].T
                transfer_t[lax.rem(c, leaves - 1)] = transfer[lax.rem(c, leaves - 1)].T
                return carry

            lax.fori_loop(0, leaves, turn_round, 0, unroll=min(UNROLL, leaves))
            x_hand_over(1)
        tiles = exchange_wait(turn + 1)
        total_square = jnp.sum(tiles, axis=0)
        if turn == 0:
            x_wait(1)
        levels.append(tiles)
        for level in range(high_levels - 1):
            half = levels[-1].shape[0] // 2
            levels.append(up_level(levels[-1], top_t[place : place + half], batched_t)[0])
            place += half
            starts.append(place)
        for level in range(low_levels, low_levels + high_levels):
            owns.append(level_links(level, levels[level], starts[level]))

        field = None
        for own, side, node in reversed(owns):
            if field is not None:
                half_lanes = pl.multiple_of(side * RANK, RANK)
                half = top_t[node, :, pl.ds(half_lanes, RANK)]
                own = own + jnp.dot(field.astype(bf16), half, preferred_element_type=f32)
            field = own
        field = both_halves(field)[None]

        for _, offset, half in reversed(saved):
            child = batched(field.astype(bf16), transfer_t[offset : offset + half])
            left = child[:, :, :RANK] + links[0, offset : offset + half]
            right = child[:, :, RANK:] + links[1, offset : offset + half]
            field = jnp.stack([left, right], axis=1).reshape(2 * half, ROWS, RANK)
        image[...] = dense[...] + batched(field.astype(bf16), basis_t[...])
        if turn > 0:
            scatter(image, 1)

        inside = jnp.zeros((ROWS, RANK), f32)
        for level in range(low_levels, low_levels + high_levels):
            inside = inside + level_product(levels[level], starts[level])
        sums = jnp.sum(exchange_wait(turn + 3), axis=0)
        sums = full(sums + jnp.where(upper, 2.0 * inside, 0.0))
        total_square = full(total_square)
        return (
            jnp.where(upper, swap(total_square), total_square),
            both_halves(sums),
            jnp.where(upper, swap(sums), sums),
        )

    load_basis.wait()
    load_transfer.wait()
    load_coupling.wait()

    rr_first, curve_first, _ = apply_matrix(0, jnp.zeros((ROWS, RANK), f32))
    step_size = rr_first / curve_first
    start = vec[...]
    product = image[...]
    first[...] = product
    residual = start - wide_of(step_size) * product
    vec[...] = residual

    rr_second, curve, cross = apply_matrix(4, lane_partial(residual * product))
    ratio = rr_second / rr_first
    last_size = rr_second / (curve + 2.0 * ratio * cross + ratio * ratio * curve_first)
    step_size, ratio, last_size = (
        jnp.concatenate([tile, tile], axis=1)[:4] for tile in (step_size, ratio, last_size)
    )

    for h in range(leaves):
        tile = acc[0, h * 8 : h * 8 + 8, :]
        image_first = (tile + swap(tile))[:4]
        tile = acc[1, h * 8 : h * 8 + 8, :]
        image_second = (tile + swap(tile))[:4]
        start = tgt_ref[:, h * LEAF : (h + 1) * LEAF]
        residual = start - step_size * image_first
        direction = residual + ratio * start
        sol_ref[:, h * LEAF : (h + 1) * LEAF] = step_size * start + last_size * direction
        product = image_second + ratio * image_first
        res_ref[:, h * LEAF : (h + 1) * LEAF] = residual - last_size * product

    for part in range(2):
        for j in far_first(spread):
            other = lax.rem(mine + j, spread)
            for copy in x_copies(part, mine, core, across, j - 1, (leaf, other)):
                copy.wait_send()
            for copy in x_copies(part, other, core, handed, j - 1, (pair, mine)):
                copy.wait_send()
    for turn in range(ROUNDS):
        me, number = (inner, group) if turn % 2 == 0 else (plane, planes)
        for j in far_first(number):
            tile_copy(turn, me, j, partner(turn, j)[1]).wait_send()


def hand_out(sol_in, res_in, sol_out, res_out, sem):
    copies = [
        pltpu.make_async_copy(sol_in, sol_out, sem.at[0]),
        pltpu.make_async_copy(res_in, res_out, sem.at[1]),
    ]
    for copy in copies:
        copy.start()
    for copy in copies:
        copy.wait()


def per_device(
    targets,
    points,
    tree_order,
    leaf_basis,
    transfer_local,
    coupling_local,
    transfer_top,
    coupling_top,
):
    spread = lax.axis_size("rhs")
    count = lax.axis_size("leaf")
    bits = count.bit_length() - 1
    group = 1 << (bits + 1) // 2
    planes = count // group
    leaves = leaf_basis.shape[0]
    columns, here = targets.shape
    nodes = group - 1 + planes - 1
    loads = 3 + 2 * (group.bit_length())
    most = max(group, planes)
    vmem = pl.BlockSpec(memory_space=pltpu.VMEM)
    any_space = pl.BlockSpec(memory_space=pl.ANY)
    hbm_space = pl.BlockSpec(memory_space=pltpu.HBM)
    out = jax.ShapeDtypeStruct((columns, here), f32)
    results = pl.pallas_call(
        functools.partial(whole_kernel, (spread, group, planes, leaves)),
        out_shape=(out, out),
        in_specs=[vmem, vmem, vmem] + [any_space] * 5,
        out_specs=(vmem, vmem),
        scratch_shapes=[
            pltpu.VMEM(leaf_basis.shape, bf16),
            pltpu.VMEM(transfer_local.shape, bf16),
            pltpu.VMEM(coupling_local.shape, bf16),
            pltpu.VMEM((nodes, RANK, 2 * RANK), bf16),
            pltpu.VMEM((nodes, RANK, RANK), bf16),
            pltpu.VMEM((leaves * 8, LEAF), f32),
            pltpu.VMEM((leaves * 8, LEAF), bf16),
            pltpu.VMEM((leaves * 16, LEAF), bf16),
            pltpu.VMEM((leaves, LEAF, LEAF), bf16),
            pltpu.VMEM((leaves, LEAF, LEAF), bf16),
            pltpu.VMEM((leaves, LEAF, LEAF), bf16),
            pltpu.VMEM((leaves, ROWS, LEAF), f32),
            pltpu.VMEM((leaves, ROWS, LEAF), f32),
            pltpu.VMEM((leaves, ROWS, LEAF), f32),
            pltpu.VMEM((leaves, ROWS, LEAF), f32),
            pltpu.VMEM((2, leaves * 8, LEAF), f32),
            pltpu.VMEM((2, leaves - 1, ROWS, RANK), f32),
            pltpu.VMEM((ROUNDS, most, ROWS, RANK), f32),
            pltpu.SemaphoreType.DMA((loads,)),
            pltpu.SemaphoreType.DMA((4, spread - 1)),
            pltpu.SemaphoreType.DMA((4, spread)),
            pltpu.SemaphoreType.DMA((4, spread - 1)),
            pltpu.SemaphoreType.DMA((4, spread)),
            pltpu.SemaphoreType.DMA((ROUNDS, most - 1)),
            pltpu.SemaphoreType.DMA((ROUNDS, most)),
            pltpu.VMEM((leaves, RANK, LEAF), bf16),
            pltpu.VMEM((leaves - 1, RANK, 2 * RANK), bf16),
        ],
        compiler_params=pltpu.CompilerParams(
            collective_id=0, has_side_effects=True, vmem_limit_bytes=56 * 1024 * 1024
        ),
        name="ridge",
    )(
        targets,
        points,
        tree_order.reshape(-1, RANK),
        leaf_basis,
        transfer_local,
        coupling_local,
        transfer_top.transpose(0, 2, 1),
        coupling_top.transpose(0, 2, 1),
    )
    return pl.pallas_call(
        hand_out,
        out_shape=(out, out),
        in_specs=[vmem, vmem],
        out_specs=(hbm_space, hbm_space),
        scratch_shapes=[pltpu.SemaphoreType.DMA((2,))],
        name="hand_out",
    )(*results)


def solution(mesh):
    placed = (
        P("rhs", "leaf"),
        P(None, "leaf"),
        P("leaf"),
        P("leaf", None, None),
        P("leaf", None, None),
        P("leaf", None, None),
        P(None, None, "rhs"),
        P(None, None, "rhs"),
    )
    return jax.shard_map(
        per_device,
        mesh=mesh,
        in_specs=placed,
        out_specs=(P("rhs", "leaf"), P("rhs", "leaf")),
        check_vma=False,
    )
```

```python
import functools

import jax
import jax.numpy as jnp
from jax import lax
from jax.experimental import pallas as pl
from jax.experimental.pallas import tpu as pltpu
from jax.sharding import PartitionSpec as P

LEAF = 256
RANK = 128
DIMS = 8
ROWS = 8
kernel_rate = 0.0625
ridge_term = 1.0

f32 = jnp.float32
bf16 = jnp.bfloat16
MESH = pl.DeviceIdType.MESH
ROUNDS = 8
UNROLL = 8


def rounded(values):
    return values.astype(bf16).astype(f32)


def batched(left, right):
    return lax.dot_general(left, right, (((2,), (1,)), ((0,), (0,))), preferred_element_type=f32)


def batched_t(left, right):
    return lax.dot_general(left, right, (((2,), (2,)), ((0,), (0,))), preferred_element_type=f32)


def up_level(coeffs, matrices, multiply=batched):
    half = coeffs.shape[0] // 2
    paired = coeffs.reshape(half, 2, ROWS, RANK)
    joined = jnp.concatenate([paired[:, 0], paired[:, 1]], axis=-1).astype(bf16)
    return rounded(multiply(joined, matrices)), paired


def whole_kernel(
    sizes,
    tgt_ref,
    pts_ref,
    idx_ref,
    basis_hbm,
    transfer_hbm,
    coupling_hbm,
    ttop_hbm,
    ctop_hbm,
    sol_ref,
    res_ref,
    basis,
    transfer,
    coupling,
    top_t,
    top_c,
    lhs_t32,
    lhs_t,
    lhs_p,
    onehot,
    k_high,
    k_low,
    vec,
    dense,
    image,
    first,
    acc,
    links,
    slots,
    load_sem,
    x_send,
    x_recv,
    h_send,
    h_recv,
    t_send,
    t_recv,
    basis_t,
    transfer_t,
):
    spread, group, planes, leaves = sizes
    leaf = lax.axis_index("leaf")
    mine = lax.axis_index("rhs")
    inner = lax.rem(leaf, group)
    plane = leaf // group
    base = plane * group

    barrier = pltpu.get_barrier_semaphore()

    def greet_inner(j, carry):
        other = base + lax.rem(inner + j, group)
        pl.semaphore_signal(barrier, inc=1, device_id=(other, mine), device_id_type=MESH)
        return carry

    def greet_plane(j, carry):
        other = inner + group * lax.rem(plane + j, planes)
        pl.semaphore_signal(barrier, inc=1, device_id=(other, mine), device_id_type=MESH)
        return carry

    def greet_x(j, carry):
        other = lax.rem(mine + j, spread)
        pl.semaphore_signal(barrier, inc=1, device_id=(leaf, other), device_id_type=MESH)
        return carry

    width = RANK // spread
    mine_rows = pl.ds(pl.multiple_of(mine * width, width), width)
    tops = []
    low_levels = group.bit_length() - 1
    high_levels = planes.bit_length() - 1
    count = group * planes
    place = 0
    first_node = 0
    for level in range(low_levels):
        here = group >> level + 1
        tops.append((first_node + plane * here, place, here))
        place += here
        first_node += count >> level + 1
    tops.append((first_node, place, planes - 1))
    place += planes - 1
    nodes = place
    top_loads = []
    for i, (source, target, number) in enumerate(tops):
        for hbm, top, k in ((ttop_hbm, top_t, 0), (ctop_hbm, top_c, 1)):
            copy = pltpu.make_async_copy(
                hbm.at[pl.ds(source, number)],
                top.at[pl.ds(target, number), mine_rows],
                load_sem.at[3 + 2 * i + k],
            )
            copy.start()
            top_loads.append(copy)
    load_basis = pltpu.make_async_copy(basis_hbm, basis, load_sem.at[0])
    load_transfer = pltpu.make_async_copy(transfer_hbm, transfer, load_sem.at[1])
    load_coupling = pltpu.make_async_copy(coupling_hbm, coupling, load_sem.at[2])
    load_basis.start()
    load_transfer.start()
    load_coupling.start()

    lax.fori_loop(1, group, greet_inner, 0)
    lax.fori_loop(1, planes, greet_plane, 0)
    lax.fori_loop(1, spread, greet_x, 0)

    for h in range(leaves):
        piece = tgt_ref[:, h * LEAF : (h + 1) * LEAF]
        high = rounded(piece)
        lhs_t32[h * 8 : h * 8 + 4, :] = high
        lhs_t32[h * 8 + 4 : h * 8 + 8, :] = piece - high
        piece = pts_ref[:, h * LEAF : (h + 1) * LEAF]
        high = rounded(piece)
        lhs_p[h * 16 : (h + 1) * 16, :] = jnp.concatenate([high, piece - high], axis=0).astype(bf16)
    lhs_t[...] = lhs_t32[...].astype(bf16)

    low_nodes = group - 1
    parts = (pl.ds(0, low_nodes), pl.ds(low_nodes, nodes - low_nodes))
    core = lax.rem(leaf, 2)
    pair = leaf + 1 - 2 * core
    half_width = width // 2

    def x_copies(part, owner, half, sems, slot, place):
        first_row = pl.multiple_of(owner * width + half * half_width, half_width)
        rows = pl.ds(first_row, half_width)
        send, recv = sems
        return [
            pltpu.make_async_remote_copy(
                src_ref=top.at[parts[part], rows],
                dst_ref=top.at[parts[part], rows],
                send_sem=send.at[2 * part + k, slot],
                recv_sem=recv.at[2 * part + k, owner],
                device_id=place,
                device_id_type=MESH,
            )
            for k, top in enumerate((top_t, top_c))
        ]

    def far_first(number):
        return sorted(range(1, number), key=lambda j: (-min(j, number - j), j))

    across, handed = (x_send, x_recv), (h_send, h_recv)

    def x_start():
        for part in range(2):
            for copy in top_loads[: 2 * low_levels] if part == 0 else top_loads[2 * low_levels :]:
                copy.wait()
            for j in far_first(spread):
                place = (leaf, lax.rem(mine + j, spread))
                for copy in x_copies(part, mine, core, across, j - 1, place):
                    copy.start()

    def x_hand_over(part):
        for j in reversed(far_first(spread)):
            other = lax.rem(mine + j, spread)
            for copy in x_copies(part, other, core, across, j - 1, (leaf, other)):
                copy.wait_recv()
            for copy in x_copies(part, other, core, handed, j - 1, (pair, mine)):
                copy.start()

    def x_wait(part):
        for j in reversed(far_first(spread)):
            other = lax.rem(mine + j, spread)
            for copy in x_copies(part, other, 1 - core, handed, j - 1, (pair, mine)):
                copy.wait_recv()

    pl.semaphore_wait(barrier, group - 1 + planes - 1 + spread - 1)
    x_start()

    def tile_copy(turn, slot, j, other):
        return pltpu.make_async_remote_copy(
            src_ref=slots.at[turn, slot],
            dst_ref=slots.at[turn, slot],
            send_sem=t_send.at[turn, j - 1],
            recv_sem=t_recv.at[turn, slot],
            device_id=(other, mine),
            device_id_type=MESH,
        )

    def partner(turn, j):
        if turn % 2 == 0:
            slot = lax.rem(inner + j, group)
            return slot, base + slot
        slot = lax.rem(plane + j, planes)
        return slot, inner + group * slot

    def exchange_start(turn, tile):
        me, number = (inner, group) if turn % 2 == 0 else (plane, planes)
        slots[turn, me] = tile
        for j in far_first(number):
            tile_copy(turn, me, j, partner(turn, j)[1]).start()

    def exchange_wait(turn):
        number = group if turn % 2 == 0 else planes
        for j in reversed(far_first(number)):
            slot, other = partner(turn, j)
            tile_copy(turn, slot, j, other).wait_recv()
        return slots[turn, :number]

    def index_row(c):
        return jnp.concatenate(
            [idx_ref[pl.ds(2 * c, 1), :], idx_ref[pl.ds(2 * c + 1, 1), :]], axis=1
        )

    def gather_leaf(c, carry):
        order = index_row(c)
        low = lax.bitwise_and(order, LEAF - 1)
        high = lax.shift_right_logical(order, 8)
        hot = lax.broadcasted_iota(jnp.int32, (LEAF, LEAF), 0) == low
        hot = jnp.where(hot, 1.0, 0.0).astype(bf16)
        onehot[c] = hot
        rows_t = jnp.dot(lhs_t[...], hot, preferred_element_type=f32).reshape(leaves, 8, LEAF)
        rows_p = jnp.dot(lhs_p[...], hot, preferred_element_type=f32).reshape(leaves, 16, LEAF)
        here = lax.broadcasted_iota(jnp.int32, (leaves, 8, LEAF), 0) == high[None]
        both = jnp.sum(jnp.where(here, rows_t, 0.0), axis=0)
        spot_high = jnp.sum(jnp.where(here, rows_p[:, :8], 0.0), axis=0)
        spot_low = jnp.sum(jnp.where(here, rows_p[:, 8:], 0.0), axis=0)
        vec[c] = both + pltpu.roll(both, 4, 0)
        whole = spot_high + spot_low
        norm = jnp.sum(whole * whole, axis=0, keepdims=True) * -kernel_rate
        norm_a = rounded(norm)
        norm_b = rounded(norm - norm_a)
        norm_c = norm - norm_a - norm_b
        row = lax.broadcasted_iota(jnp.int32, (8, LEAF), 0)
        norms = jnp.where(row == 0, norm_a, jnp.where(row == 1, norm_b, norm_c))
        ones = jnp.ones((8, LEAF), f32)
        zeros = jnp.zeros((8, LEAF), f32)
        tail_left = jnp.where(row < 3, norms, jnp.where(row < 6, ones, zeros))
        norms_up = jnp.where(row == 3, norm_a, jnp.where(row == 4, norm_b, norm_c))
        tail_right = jnp.where(row < 3, ones, jnp.where(row < 6, norms_up, zeros))
        left = jnp.concatenate(
            [spot_high, spot_high, spot_low, spot_low, tail_left, zeros], axis=0
        ).astype(bf16)
        right_high = spot_high * (2 * kernel_rate)
        right_low = spot_low * (2 * kernel_rate)
        right = jnp.concatenate(
            [right_high, right_low, right_high, right_low, tail_right, zeros], axis=0
        ).astype(bf16)
        power = lax.dot_general(left, right, (((0,), (0,)), ((), ())), preferred_element_type=f32)
        values = jnp.exp(power)
        values_high = values.astype(bf16)
        k_high[c] = values_high
        k_low[c] = (values - values_high.astype(f32)).astype(bf16)
        return carry

    lax.fori_loop(0, leaves, gather_leaf, 0, unroll=min(2 * UNROLL, leaves))

    row8 = lax.broadcasted_iota(jnp.int32, (ROWS, RANK), 0)
    upper = row8 < 4

    def swap(tile):
        return pltpu.roll(tile, 4, 0)

    def lane_partial(product):
        total = jnp.sum(product, axis=0)
        return total[:, :RANK] + total[:, RANK:]

    def full(tile):
        return jnp.broadcast_to(jnp.sum(tile, axis=1, keepdims=True), (ROWS, RANK))

    def wide_of(tile):
        return jnp.concatenate([tile, tile], axis=1)[None]

    def both_halves(tile):
        return jnp.where(upper, tile, swap(tile))

    def level_links(level, pairs, place):
        spot, depth = (plane, level - low_levels) if level >= low_levels else (inner, level)
        node = lax.shift_right_logical(spot, depth + 1)
        side = lax.bitwise_and(lax.shift_right_logical(spot, depth), 1)
        sibling = jnp.zeros((ROWS, RANK), f32)
        for k in range(pairs.shape[0]):
            chosen = lax.shift_right_logical(spot, depth) + 1 - 2 * side == k
            sibling = jnp.where(chosen, pairs[k], sibling)
        sibling = sibling.astype(bf16)
        link = top_c[place + node]
        to_left = jnp.dot(sibling, link, preferred_element_type=f32)
        to_right = lax.dot_general(
            sibling, link, (((1,), (1,)), ((), ())), preferred_element_type=f32
        )
        return jnp.where(side == 0, to_left, to_right), side, place + node

    def level_product(pairs, place):
        half = pairs.shape[0] // 2
        paired = pairs.reshape(half, 2, ROWS, RANK)
        toward = batched(paired[:, 1].astype(bf16), top_c[place : place + half])
        return jnp.sum(paired[:, 0] * toward, axis=0)

    def scatter(source, k):
        sub_row = lax.broadcasted_iota(jnp.int32, (ROWS, LEAF), 0)
        inner_steps = min(2 * UNROLL, leaves)

        def step(i, carry):
            total = jnp.zeros((leaves * 8, LEAF), f32)
            for t in range(inner_steps):
                c = i * inner_steps + t
                high = lax.shift_right_logical(index_row(c), 8)
                here = lax.broadcasted_iota(jnp.int32, (leaves, 8, LEAF), 0) == high[None]
                value = source[c]
                value_high = rounded(value)
                pieces = jnp.where(sub_row < 4, value_high, value - value_high)
                rows = jnp.where(here, pieces[None], 0.0).reshape(leaves * 8, LEAF).astype(bf16)
                total = total + lax.dot_general(
                    rows, onehot[c], (((1,), (1,)), ((), ())), preferred_element_type=f32
                )
            acc[k] += total
            return carry

        acc[k] = jnp.zeros((leaves * 8, LEAF), f32)
        lax.fori_loop(0, leaves // inner_steps, step, 0)

    def apply_matrix(turn, extra):
        value = vec[...]
        square = lane_partial(value * value)
        coeffs = rounded(batched(value.astype(bf16), basis[...]))
        saved = []
        offset = 0
        number = leaves
        while number > 1:
            half = number // 2
            coeffs, paired = up_level(coeffs, transfer[offset : offset + half])
            saved.append((paired, offset, half))
            offset += half
            number = half
        exchange_start(turn, jnp.where(upper, coeffs[0], square))

        high = rounded(value)
        sub_row = lax.broadcasted_iota(jnp.int32, value.shape, 1)
        stacked = jnp.where(sub_row < 4, high, value - high).astype(bf16)
        product = batched(stacked, k_high[...]) + batched(stacked, k_low[...])
        product = product + pltpu.roll(product, 4, 1) + ridge_term * value
        dense[...] = product
        inside = jnp.zeros((ROWS, RANK), f32)
        for paired, offset, half in saved:
            matrices = coupling[offset : offset + half]
            toward = batched_t(paired[:, 1].astype(bf16), matrices)
            links[0, offset : offset + half] = toward
            links[1, offset : offset + half] = batched(paired[:, 0].astype(bf16), matrices)
            inside = inside + jnp.sum(paired[:, 0] * toward, axis=0)
        inside = 2.0 * inside + lane_partial(value * product)
        exchange_start(turn + 2, jnp.where(upper, inside, extra))

        if turn == 0:
            x_hand_over(0)
        tiles = exchange_wait(turn)
        group_square = jnp.sum(tiles, axis=0)
        if turn == 0:
            x_wait(0)
        levels = [tiles]
        starts = [0]
        place = 0
        for level in range(low_levels):
            half = levels[-1].shape[0] // 2
            levels.append(up_level(levels[-1], top_t[place : place + half], batched_t)[0])
            place += half
            starts.append(place)
        exchange_start(turn + 1, jnp.where(upper, levels.pop()[0], group_square))

        owns = [level_links(level, levels[level], starts[level]) for level in range(low_levels)]
        inside = jnp.zeros((ROWS, RANK), f32)
        for level in range(low_levels):
            inside = inside + level_product(levels[level], starts[level])
        if turn > 0:
            scatter(first, 0)
        group_sums = jnp.sum(exchange_wait(turn + 2), axis=0)
        exchange_start(turn + 3, group_sums + jnp.where(upper, 2.0 * inside, 0.0))

        if turn == 0:
            def turn_round(c, carry):
                basis_t[c] = basis[c].T
                transfer_t[lax.rem(c, leaves - 1)] = transfer[lax.rem(c, leaves - 1)].T
                return carry

            lax.fori_loop(0, leaves, turn_round, 0, unroll=min(UNROLL, leaves))
            x_hand_over(1)
        tiles = exchange_wait(turn + 1)
        total_square = jnp.sum(tiles, axis=0)
        if turn == 0:
            x_wait(1)
        levels.append(tiles)
        for level in range(high_levels - 1):
            half = levels[-1].shape[0] // 2
            levels.append(up_level(levels[-1], top_t[place : place + half], batched_t)[0])
            place += half
            starts.append(place)
        for level in range(low_levels, low_levels + high_levels):
            owns.append(level_links(level, levels[level], starts[level]))

        inside = jnp.zeros((ROWS, RANK), f32)
        for level in range(low_levels, low_levels + high_levels):
            inside = inside + level_product(levels[level], starts[level])

        field = None
        for own, side, node in reversed(owns):
            if field is not None:
                half_lanes = pl.multiple_of(side * RANK, RANK)
                half = top_t[node, :, pl.ds(half_lanes, RANK)]
                own = own + jnp.dot(field.astype(bf16), half, preferred_element_type=f32)
            field = own
        field = both_halves(field)[None]

        for _, offset, half in reversed(saved):
            child = batched(field.astype(bf16), transfer_t[offset : offset + half])
            left = child[:, :, :RANK] + links[0, offset : offset + half]
            right = child[:, :, RANK:] + links[1, offset : offset + half]
            field = jnp.stack([left, right], axis=1).reshape(2 * half, ROWS, RANK)
        image[...] = dense[...] + batched(field.astype(bf16), basis_t[...])
        if turn > 0:
            scatter(image, 1)

        sums = jnp.sum(exchange_wait(turn + 3), axis=0)
        sums = full(sums + jnp.where(upper, 2.0 * inside, 0.0))
        total_square = full(total_square)
        return (
            jnp.where(upper, swap(total_square), total_square),
            both_halves(sums),
            jnp.where(upper, swap(sums), sums),
        )

    load_basis.wait()
    load_transfer.wait()
    load_coupling.wait()

    rr_first, curve_first, _ = apply_matrix(0, jnp.zeros((ROWS, RANK), f32))
    step_size = rr_first / curve_first
    start = vec[...]
    product = image[...]
    first[...] = product
    residual = start - wide_of(step_size) * product
    vec[...] = residual

    rr_second, curve, cross = apply_matrix(4, lane_partial(residual * product))
    ratio = rr_second / rr_first
    last_size = rr_second / (curve + 2.0 * ratio * cross + ratio * ratio * curve_first)
    step_size, ratio, last_size = (
        jnp.concatenate([tile, tile], axis=1)[:4] for tile in (step_size, ratio, last_size)
    )

    for h in range(leaves):
        tile = acc[0, h * 8 : h * 8 + 8, :]
        image_first = (tile + swap(tile))[:4]
        tile = acc[1, h * 8 : h * 8 + 8, :]
        image_second = (tile + swap(tile))[:4]
        start = tgt_ref[:, h * LEAF : (h + 1) * LEAF]
        residual = start - step_size * image_first
        direction = residual + ratio * start
        sol_ref[:, h * LEAF : (h + 1) * LEAF] = step_size * start + last_size * direction
        product = image_second + ratio * image_first
        res_ref[:, h * LEAF : (h + 1) * LEAF] = residual - last_size * product

    for part in range(2):
        for j in far_first(spread):
            other = lax.rem(mine + j, spread)
            for copy in x_copies(part, mine, core, across, j - 1, (leaf, other)):
                copy.wait_send()
            for copy in x_copies(part, other, core, handed, j - 1, (pair, mine)):
                copy.wait_send()
    for turn in range(ROUNDS):
        me, number = (inner, group) if turn % 2 == 0 else (plane, planes)
        for j in far_first(number):
            tile_copy(turn, me, j, partner(turn, j)[1]).wait_send()


def hand_out(sol_in, res_in, sol_out, res_out, sem):
    copies = [
        pltpu.make_async_copy(sol_in, sol_out, sem.at[0]),
        pltpu.make_async_copy(res_in, res_out, sem.at[1]),
    ]
    for copy in copies:
        copy.start()
    for copy in copies:
        copy.wait()


def per_device(
    targets,
    points,
    tree_order,
    leaf_basis,
    transfer_local,
    coupling_local,
    transfer_top,
    coupling_top,
):
    spread = lax.axis_size("rhs")
    count = lax.axis_size("leaf")
    bits = count.bit_length() - 1
    group = 1 << (bits + 1) // 2
    planes = count // group
    leaves = leaf_basis.shape[0]
    columns, here = targets.shape
    nodes = group - 1 + planes - 1
    loads = 3 + 2 * (group.bit_length())
    most = max(group, planes)
    vmem = pl.BlockSpec(memory_space=pltpu.VMEM)
    any_space = pl.BlockSpec(memory_space=pl.ANY)
    hbm_space = pl.BlockSpec(memory_space=pltpu.HBM)
    out = jax.ShapeDtypeStruct((columns, here), f32)
    results = pl.pallas_call(
        functools.partial(whole_kernel, (spread, group, planes, leaves)),
        out_shape=(out, out),
        in_specs=[vmem, vmem, vmem] + [any_space] * 5,
        out_specs=(vmem, vmem),
        scratch_shapes=[
            pltpu.VMEM(leaf_basis.shape, bf16),
            pltpu.VMEM(transfer_local.shape, bf16),
            pltpu.VMEM(coupling_local.shape, bf16),
            pltpu.VMEM((nodes, RANK, 2 * RANK), bf16),
            pltpu.VMEM((nodes, RANK, RANK), bf16),
            pltpu.VMEM((leaves * 8, LEAF), f32),
            pltpu.VMEM((leaves * 8, LEAF), bf16),
            pltpu.VMEM((leaves * 16, LEAF), bf16),
            pltpu.VMEM((leaves, LEAF, LEAF), bf16),
            pltpu.VMEM((leaves, LEAF, LEAF), bf16),
            pltpu.VMEM((leaves, LEAF, LEAF), bf16),
            pltpu.VMEM((leaves, ROWS, LEAF), f32),
            pltpu.VMEM((leaves, ROWS, LEAF), f32),
            pltpu.VMEM((leaves, ROWS, LEAF), f32),
            pltpu.VMEM((leaves, ROWS, LEAF), f32),
            pltpu.VMEM((2, leaves * 8, LEAF), f32),
            pltpu.VMEM((2, leaves - 1, ROWS, RANK), f32),
            pltpu.VMEM((ROUNDS, most, ROWS, RANK), f32),
            pltpu.SemaphoreType.DMA((loads,)),
            pltpu.SemaphoreType.DMA((4, spread - 1)),
            pltpu.SemaphoreType.DMA((4, spread)),
            pltpu.SemaphoreType.DMA((4, spread - 1)),
            pltpu.SemaphoreType.DMA((4, spread)),
            pltpu.SemaphoreType.DMA((ROUNDS, most - 1)),
            pltpu.SemaphoreType.DMA((ROUNDS, most)),
            pltpu.VMEM((leaves, RANK, LEAF), bf16),
            pltpu.VMEM((leaves - 1, RANK, 2 * RANK), bf16),
        ],
        compiler_params=pltpu.CompilerParams(
            collective_id=0, has_side_effects=True, vmem_limit_bytes=56 * 1024 * 1024
        ),
        name="ridge",
    )(
        targets,
        points,
        tree_order.reshape(-1, RANK),
        leaf_basis,
        transfer_local,
        coupling_local,
        transfer_top.transpose(0, 2, 1),
        coupling_top.transpose(0, 2, 1),
    )
    return pl.pallas_call(
        hand_out,
        out_shape=(out, out),
        in_specs=[vmem, vmem],
        out_specs=(hbm_space, hbm_space),
        scratch_shapes=[pltpu.SemaphoreType.DMA((2,))],
        name="hand_out",
    )(*results)


def solution(mesh):
    placed = (
        P("rhs", "leaf"),
        P(None, "leaf"),
        P("leaf"),
        P("leaf", None, None),
        P("leaf", None, None),
        P("leaf", None, None),
        P(None, None, "rhs"),
        P(None, None, "rhs"),
    )
    return jax.shard_map(
        per_device,
        mesh=mesh,
        in_specs=placed,
        out_specs=(P("rhs", "leaf"), P("rhs", "leaf")),
        check_vma=False,
    )
```

```python
import functools

import jax
import jax.numpy as jnp
from jax import lax
from jax.experimental import pallas as pl
from jax.experimental.pallas import tpu as pltpu
from jax.sharding import PartitionSpec as P

LEAF = 256
RANK = 128
DIMS = 8
ROWS = 8
kernel_rate = 0.0625
ridge_term = 1.0

f32 = jnp.float32
bf16 = jnp.bfloat16
MESH = pl.DeviceIdType.MESH
ROUNDS = 8
UNROLL = 8


def rounded(values):
    return values.astype(bf16).astype(f32)


def batched(left, right):
    return lax.dot_general(left, right, (((2,), (1,)), ((0,), (0,))), preferred_element_type=f32)


def batched_t(left, right):
    return lax.dot_general(left, right, (((2,), (2,)), ((0,), (0,))), preferred_element_type=f32)


def up_level(coeffs, matrices, multiply=batched):
    half = coeffs.shape[0] // 2
    paired = coeffs.reshape(half, 2, ROWS, RANK)
    joined = jnp.concatenate([paired[:, 0], paired[:, 1]], axis=-1).astype(bf16)
    return rounded(multiply(joined, matrices)), paired


def whole_kernel(
    sizes,
    tgt_ref,
    pts_ref,
    idx_ref,
    basis_hbm,
    transfer_hbm,
    coupling_hbm,
    ttop_hbm,
    ctop_hbm,
    sol_ref,
    res_ref,
    basis,
    transfer,
    coupling,
    top_t,
    top_c,
    lhs_t32,
    lhs_t,
    lhs_p,
    onehot,
    k_high,
    k_low,
    vec,
    dense,
    image,
    first,
    acc,
    links,
    slots,
    load_sem,
    x_send,
    x_recv,
    h_send,
    h_recv,
    t_send,
    t_recv,
    basis_t,
    transfer_t,
):
    spread, group, planes, leaves = sizes
    leaf = lax.axis_index("leaf")
    mine = lax.axis_index("rhs")
    inner = lax.rem(leaf, group)
    plane = leaf // group
    base = plane * group

    barrier = pltpu.get_barrier_semaphore()

    def greet_inner(j, carry):
        other = base + lax.rem(inner + j, group)
        pl.semaphore_signal(barrier, inc=1, device_id=(other, mine), device_id_type=MESH)
        return carry

    def greet_plane(j, carry):
        other = inner + group * lax.rem(plane + j, planes)
        pl.semaphore_signal(barrier, inc=1, device_id=(other, mine), device_id_type=MESH)
        return carry

    def greet_x(j, carry):
        other = lax.rem(mine + j, spread)
        pl.semaphore_signal(barrier, inc=1, device_id=(leaf, other), device_id_type=MESH)
        return carry

    width = RANK // spread
    mine_rows = pl.ds(pl.multiple_of(mine * width, width), width)
    tops = []
    low_levels = group.bit_length() - 1
    high_levels = planes.bit_length() - 1
    count = group * planes
    place = 0
    first_node = 0
    for level in range(low_levels):
        here = group >> level + 1
        tops.append((first_node + plane * here, place, here))
        place += here
        first_node += count >> level + 1
    tops.append((first_node, place, planes - 1))
    place += planes - 1
    nodes = place
    top_loads = []
    for i, (source, target, number) in enumerate(tops):
        for hbm, top, k in ((ttop_hbm, top_t, 0), (ctop_hbm, top_c, 1)):
            copy = pltpu.make_async_copy(
                hbm.at[pl.ds(source, number)],
                top.at[pl.ds(target, number), mine_rows],
                load_sem.at[3 + 2 * i + k],
            )
            copy.start()
            top_loads.append(copy)
    load_basis = pltpu.make_async_copy(basis_hbm, basis, load_sem.at[0])
    load_transfer = pltpu.make_async_copy(transfer_hbm, transfer, load_sem.at[1])
    load_coupling = pltpu.make_async_copy(coupling_hbm, coupling, load_sem.at[2])
    load_basis.start()
    load_transfer.start()
    load_coupling.start()

    lax.fori_loop(1, group, greet_inner, 0)
    lax.fori_loop(1, planes, greet_plane, 0)
    lax.fori_loop(1, spread, greet_x, 0)

    for h in range(leaves):
        piece = tgt_ref[:, h * LEAF : (h + 1) * LEAF]
        high = rounded(piece)
        lhs_t32[h * 8 : h * 8 + 4, :] = high
        lhs_t32[h * 8 + 4 : h * 8 + 8, :] = piece - high
        piece = pts_ref[:, h * LEAF : (h + 1) * LEAF]
        high = rounded(piece)
        lhs_p[h * 16 : (h + 1) * 16, :] = jnp.concatenate([high, piece - high], axis=0).astype(bf16)
    lhs_t[...] = lhs_t32[...].astype(bf16)

    low_nodes = group - 1
    parts = (pl.ds(0, low_nodes), pl.ds(low_nodes, nodes - low_nodes))
    core = lax.rem(leaf, 2)
    pair = leaf + 1 - 2 * core
    half_width = width // 2

    def x_copies(part, owner, half, sems, slot, place):
        first_row = pl.multiple_of(owner * width + half * half_width, half_width)
        rows = pl.ds(first_row, half_width)
        send, recv = sems
        return [
            pltpu.make_async_remote_copy(
                src_ref=top.at[parts[part], rows],
                dst_ref=top.at[parts[part], rows],
                send_sem=send.at[2 * part + k, slot],
                recv_sem=recv.at[2 * part + k, owner],
                device_id=place,
                device_id_type=MESH,
            )
            for k, top in enumerate((top_t, top_c))
        ]

    def far_first(number):
        return sorted(range(1, number), key=lambda j: (-min(j, number - j), j))

    across, handed = (x_send, x_recv), (h_send, h_recv)

    def x_start():
        for part in range(2):
            for copy in top_loads[: 2 * low_levels] if part == 0 else top_loads[2 * low_levels :]:
                copy.wait()
            for j in far_first(spread):
                place = (leaf, lax.rem(mine + j, spread))
                for copy in x_copies(part, mine, core, across, j - 1, place):
                    copy.start()

    def x_hand_over(part):
        for j in reversed(far_first(spread)):
            other = lax.rem(mine + j, spread)
            for copy in x_copies(part, other, core, across, j - 1, (leaf, other)):
                copy.wait_recv()
            for copy in x_copies(part, other, core, handed, j - 1, (pair, mine)):
                copy.start()

    def x_wait(part):
        for j in reversed(far_first(spread)):
            other = lax.rem(mine + j, spread)
            for copy in x_copies(part, other, 1 - core, handed, j - 1, (pair, mine)):
                copy.wait_recv()

    pl.semaphore_wait(barrier, group - 1 + planes - 1 + spread - 1)
    x_start()

    def tile_copy(turn, slot, j, other):
        return pltpu.make_async_remote_copy(
            src_ref=slots.at[turn, slot],
            dst_ref=slots.at[turn, slot],
            send_sem=t_send.at[turn, j - 1],
            recv_sem=t_recv.at[turn, slot],
            device_id=(other, mine),
            device_id_type=MESH,
        )

    def partner(turn, j):
        if turn % 2 == 0:
            slot = lax.rem(inner + j, group)
            return slot, base + slot
        slot = lax.rem(plane + j, planes)
        return slot, inner + group * slot

    def exchange_start(turn, tile):
        me, number = (inner, group) if turn % 2 == 0 else (plane, planes)
        slots[turn, me] = tile
        for j in far_first(number):
            tile_copy(turn, me, j, partner(turn, j)[1]).start()

    def exchange_wait(turn):
        number = group if turn % 2 == 0 else planes
        for j in reversed(far_first(number)):
            slot, other = partner(turn, j)
            tile_copy(turn, slot, j, other).wait_recv()
        return slots[turn, :number]

    def index_row(c):
        return jnp.concatenate(
            [idx_ref[pl.ds(2 * c, 1), :], idx_ref[pl.ds(2 * c + 1, 1), :]], axis=1
        )

    def gather_leaf(c, carry):
        order = index_row(c)
        low = lax.bitwise_and(order, LEAF - 1)
        high = lax.shift_right_logical(order, 8)
        hot = lax.broadcasted_iota(jnp.int32, (LEAF, LEAF), 0) == low
        hot = jnp.where(hot, 1.0, 0.0).astype(bf16)
        onehot[c] = hot
        rows_t = jnp.dot(lhs_t[...], hot, preferred_element_type=f32).reshape(leaves, 8, LEAF)
        rows_p = jnp.dot(lhs_p[...], hot, preferred_element_type=f32).reshape(leaves, 16, LEAF)
        here = lax.broadcasted_iota(jnp.int32, (leaves, 8, LEAF), 0) == high[None]
        both = jnp.sum(jnp.where(here, rows_t, 0.0), axis=0)
        spot_high = jnp.sum(jnp.where(here, rows_p[:, :8], 0.0), axis=0)
        spot_low = jnp.sum(jnp.where(here, rows_p[:, 8:], 0.0), axis=0)
        vec[c] = both + pltpu.roll(both, 4, 0)
        whole = spot_high + spot_low
        norm = jnp.sum(whole * whole, axis=0, keepdims=True) * -kernel_rate
        norm_a = rounded(norm)
        norm_b = rounded(norm - norm_a)
        norm_c = norm - norm_a - norm_b
        row = lax.broadcasted_iota(jnp.int32, (8, LEAF), 0)
        norms = jnp.where(row == 0, norm_a, jnp.where(row == 1, norm_b, norm_c))
        ones = jnp.ones((8, LEAF), f32)
        zeros = jnp.zeros((8, LEAF), f32)
        tail_left = jnp.where(row < 3, norms, jnp.where(row < 6, ones, zeros))
        norms_up = jnp.where(row == 3, norm_a, jnp.where(row == 4, norm_b, norm_c))
        tail_right = jnp.where(row < 3, ones, jnp.where(row < 6, norms_up, zeros))
        left = jnp.concatenate(
            [spot_high, spot_high, spot_low, spot_low, tail_left, zeros], axis=0
        ).astype(bf16)
        right_high = spot_high * (2 * kernel_rate)
        right_low = spot_low * (2 * kernel_rate)
        right = jnp.concatenate(
            [right_high, right_low, right_high, right_low, tail_right, zeros], axis=0
        ).astype(bf16)
        power = lax.dot_general(left, right, (((0,), (0,)), ((), ())), preferred_element_type=f32)
        values = jnp.exp(power)
        values_high = values.astype(bf16)
        k_high[c] = values_high
        k_low[c] = (values - values_high.astype(f32)).astype(bf16)
        return carry

    lax.fori_loop(0, leaves, gather_leaf, 0, unroll=min(2 * UNROLL, leaves))

    row8 = lax.broadcasted_iota(jnp.int32, (ROWS, RANK), 0)
    upper = row8 < 4

    def swap(tile):
        return pltpu.roll(tile, 4, 0)

    def lane_partial(product):
        total = jnp.sum(product, axis=0)
        return total[:, :RANK] + total[:, RANK:]

    def full(tile):
        return jnp.broadcast_to(jnp.sum(tile, axis=1, keepdims=True), (ROWS, RANK))

    def wide_of(tile):
        return jnp.concatenate([tile, tile], axis=1)[None]

    def both_halves(tile):
        return jnp.where(upper, tile, swap(tile))

    def level_links(level, pairs, place):
        spot, depth = (plane, level - low_levels) if level >= low_levels else (inner, level)
        node = lax.shift_right_logical(spot, depth + 1)
        side = lax.bitwise_and(lax.shift_right_logical(spot, depth), 1)
        sibling = jnp.zeros((ROWS, RANK), f32)
        for k in range(pairs.shape[0]):
            chosen = lax.shift_right_logical(spot, depth) + 1 - 2 * side == k
            sibling = jnp.where(chosen, pairs[k], sibling)
        sibling = sibling.astype(bf16)
        link = top_c[place + node]
        to_left = jnp.dot(sibling, link, preferred_element_type=f32)
        to_right = lax.dot_general(
            sibling, link, (((1,), (1,)), ((), ())), preferred_element_type=f32
        )
        return jnp.where(side == 0, to_left, to_right), side, place + node

    def level_product(pairs, place):
        half = pairs.shape[0] // 2
        paired = pairs.reshape(half, 2, ROWS, RANK)
        toward = batched(paired[:, 1].astype(bf16), top_c[place : place + half])
        return jnp.sum(paired[:, 0] * toward, axis=0)

    def scatter(source, k):
        sub_row = lax.broadcasted_iota(jnp.int32, (ROWS, LEAF), 0)
        inner_steps = min(2 * UNROLL, leaves)

        def step(i, carry):
            total = jnp.zeros((leaves * 8, LEAF), f32)
            for t in range(inner_steps):
                c = i * inner_steps + t
                high = lax.shift_right_logical(index_row(c), 8)
                here = lax.broadcasted_iota(jnp.int32, (leaves, 8, LEAF), 0) == high[None]
                value = source[c]
                value_high = rounded(value)
                pieces = jnp.where(sub_row < 4, value_high, value - value_high)
                rows = jnp.where(here, pieces[None], 0.0).reshape(leaves * 8, LEAF).astype(bf16)
                total = total + lax.dot_general(
                    rows, onehot[c], (((1,), (1,)), ((), ())), preferred_element_type=f32
                )
            acc[k] += total
            return carry

        acc[k] = jnp.zeros((leaves * 8, LEAF), f32)
        lax.fori_loop(0, leaves // inner_steps, step, 0)

    def apply_matrix(turn, extra):
        value = vec[...]
        square = lane_partial(value * value)
        coeffs = rounded(batched(value.astype(bf16), basis[...]))
        saved = []
        offset = 0
        number = leaves
        while number > 1:
            half = number // 2
            coeffs, paired = up_level(coeffs, transfer[offset : offset + half])
            saved.append((paired, offset, half))
            offset += half
            number = half
        exchange_start(turn, jnp.where(upper, coeffs[0], square))

        high = rounded(value)
        sub_row = lax.broadcasted_iota(jnp.int32, value.shape, 1)
        stacked = jnp.where(sub_row < 4, high, value - high).astype(bf16)
        product = batched(stacked, k_high[...]) + batched(stacked, k_low[...])
        product = product + pltpu.roll(product, 4, 1) + ridge_term * value
        dense[...] = product
        inside = jnp.zeros((ROWS, RANK), f32)
        for paired, offset, half in saved:
            matrices = coupling[offset : offset + half]
            toward = batched_t(paired[:, 1].astype(bf16), matrices)
            links[0, offset : offset + half] = toward
            links[1, offset : offset + half] = batched(paired[:, 0].astype(bf16), matrices)
            inside = inside + jnp.sum(paired[:, 0] * toward, axis=0)
        inside = 2.0 * inside + lane_partial(value * product)
        exchange_start(turn + 2, jnp.where(upper, inside, extra))

        if turn == 0:
            x_hand_over(0)
        tiles = exchange_wait(turn)
        group_square = jnp.sum(tiles, axis=0)
        if turn == 0:
            x_wait(0)
        levels = [tiles]
        starts = [0]
        place = 0
        for level in range(low_levels):
            half = levels[-1].shape[0] // 2
            levels.append(up_level(levels[-1], top_t[place : place + half], batched_t)[0])
            place += half
            starts.append(place)
        exchange_start(turn + 1, jnp.where(upper, levels.pop()[0], group_square))

        owns = [level_links(level, levels[level], starts[level]) for level in range(low_levels)]
        inside = jnp.zeros((ROWS, RANK), f32)
        for level in range(low_levels):
            inside = inside + level_product(levels[level], starts[level])
        if turn > 0:
            scatter(first, 0)
        group_sums = jnp.sum(exchange_wait(turn + 2), axis=0)
        exchange_start(turn + 3, group_sums + jnp.where(upper, 2.0 * inside, 0.0))

        if turn == 0:
            def turn_round(c, carry):
                basis_t[c] = basis[c].T
                transfer_t[lax.rem(c, leaves - 1)] = transfer[lax.rem(c, leaves - 1)].T
                return carry

            lax.fori_loop(0, leaves, turn_round, 0, unroll=min(UNROLL, leaves))
            x_hand_over(1)
        tiles = exchange_wait(turn + 1)
        total_square = jnp.sum(tiles, axis=0)
        if turn == 0:
            x_wait(1)
        levels.append(tiles)
        for level in range(high_levels - 1):
            half = levels[-1].shape[0] // 2
            levels.append(up_level(levels[-1], top_t[place : place + half], batched_t)[0])
            place += half
            starts.append(place)
        for level in range(low_levels, low_levels + high_levels):
            owns.append(level_links(level, levels[level], starts[level]))

        inside = jnp.zeros((ROWS, RANK), f32)
        for level in range(low_levels, low_levels + high_levels):
            inside = inside + level_product(levels[level], starts[level])

        field = None
        for own, side, node in reversed(owns):
            if field is not None:
                half_lanes = pl.multiple_of(side * RANK, RANK)
                half = top_t[node, :, pl.ds(half_lanes, RANK)]
                own = own + jnp.dot(field.astype(bf16), half, preferred_element_type=f32)
            field = own
        field = both_halves(field)[None]

        for _, offset, half in reversed(saved):
            child = batched(field.astype(bf16), transfer_t[offset : offset + half])
            left = child[:, :, :RANK] + links[0, offset : offset + half]
            right = child[:, :, RANK:] + links[1, offset : offset + half]
            field = jnp.stack([left, right], axis=1).reshape(2 * half, ROWS, RANK)
        image[...] = dense[...] + batched(field.astype(bf16), basis_t[...])
        if turn > 0:
            scatter(image, 1)

        sums = jnp.sum(exchange_wait(turn + 3), axis=0)
        sums = full(sums + jnp.where(upper, 2.0 * inside, 0.0))
        total_square = full(total_square)
        return (
            jnp.where(upper, swap(total_square), total_square),
            both_halves(sums),
            jnp.where(upper, swap(sums), sums),
        )

    load_basis.wait()
    load_transfer.wait()
    load_coupling.wait()

    rr_first, curve_first, _ = apply_matrix(0, jnp.zeros((ROWS, RANK), f32))
    step_size = rr_first / curve_first
    start = vec[...]
    product = image[...]
    first[...] = product
    residual = start - wide_of(step_size) * product
    vec[...] = residual

    rr_second, curve, cross = apply_matrix(4, lane_partial(residual * product))
    ratio = rr_second / rr_first
    last_size = rr_second / (curve + 2.0 * ratio * cross + ratio * ratio * curve_first)
    step_size, ratio, last_size = (
        jnp.concatenate([tile, tile], axis=1)[:4] for tile in (step_size, ratio, last_size)
    )

    for h in range(leaves):
        tile = acc[0, h * 8 : h * 8 + 8, :]
        image_first = (tile + swap(tile))[:4]
        tile = acc[1, h * 8 : h * 8 + 8, :]
        image_second = (tile + swap(tile))[:4]
        start = tgt_ref[:, h * LEAF : (h + 1) * LEAF]
        residual = start - step_size * image_first
        direction = residual + ratio * start
        sol_ref[:, h * LEAF : (h + 1) * LEAF] = step_size * start + last_size * direction
        product = image_second + ratio * image_first
        res_ref[:, h * LEAF : (h + 1) * LEAF] = residual - last_size * product

    for part in range(2):
        for j in far_first(spread):
            other = lax.rem(mine + j, spread)
            for copy in x_copies(part, mine, core, across, j - 1, (leaf, other)):
                copy.wait_send()
            for copy in x_copies(part, other, core, handed, j - 1, (pair, mine)):
                copy.wait_send()
    for turn in range(ROUNDS):
        me, number = (inner, group) if turn % 2 == 0 else (plane, planes)
        for j in far_first(number):
            tile_copy(turn, me, j, partner(turn, j)[1]).wait_send()


def hand_out(sol_in, res_in, sol_out, res_out, held, sem):
    arrive = [
        pltpu.make_async_copy(source, held.at[k], sem.at[k])
        for k, source in enumerate((sol_in, res_in))
    ]
    leave = [
        pltpu.make_async_copy(held.at[k], target, sem.at[2 + k])
        for k, target in enumerate((sol_out, res_out))
    ]
    for copy in arrive:
        copy.start()
    for before, after in zip(arrive, leave):
        before.wait()
        after.start()
    for copy in leave:
        copy.wait()


def per_device(
    targets,
    points,
    tree_order,
    leaf_basis,
    transfer_local,
    coupling_local,
    transfer_top,
    coupling_top,
):
    spread = lax.axis_size("rhs")
    count = lax.axis_size("leaf")
    bits = count.bit_length() - 1
    group = 1 << (bits + 1) // 2
    planes = count // group
    leaves = leaf_basis.shape[0]
    columns, here = targets.shape
    nodes = group - 1 + planes - 1
    loads = 3 + 2 * (group.bit_length())
    most = max(group, planes)
    vmem = pl.BlockSpec(memory_space=pltpu.VMEM)
    any_space = pl.BlockSpec(memory_space=pl.ANY)
    hbm_space = pl.BlockSpec(memory_space=pltpu.HBM)
    out = jax.ShapeDtypeStruct((columns, here), f32)
    results = pl.pallas_call(
        functools.partial(whole_kernel, (spread, group, planes, leaves)),
        out_shape=(out, out),
        in_specs=[vmem, vmem, vmem] + [any_space] * 5,
        out_specs=(vmem, vmem),
        scratch_shapes=[
            pltpu.VMEM(leaf_basis.shape, bf16),
            pltpu.VMEM(transfer_local.shape, bf16),
            pltpu.VMEM(coupling_local.shape, bf16),
            pltpu.VMEM((nodes, RANK, 2 * RANK), bf16),
            pltpu.VMEM((nodes, RANK, RANK), bf16),
            pltpu.VMEM((leaves * 8, LEAF), f32),
            pltpu.VMEM((leaves * 8, LEAF), bf16),
            pltpu.VMEM((leaves * 16, LEAF), bf16),
            pltpu.VMEM((leaves, LEAF, LEAF), bf16),
            pltpu.VMEM((leaves, LEAF, LEAF), bf16),
            pltpu.VMEM((leaves, LEAF, LEAF), bf16),
            pltpu.VMEM((leaves, ROWS, LEAF), f32),
            pltpu.VMEM((leaves, ROWS, LEAF), f32),
            pltpu.VMEM((leaves, ROWS, LEAF), f32),
            pltpu.VMEM((leaves, ROWS, LEAF), f32),
            pltpu.VMEM((2, leaves * 8, LEAF), f32),
            pltpu.VMEM((2, leaves - 1, ROWS, RANK), f32),
            pltpu.VMEM((ROUNDS, most, ROWS, RANK), f32),
            pltpu.SemaphoreType.DMA((loads,)),
            pltpu.SemaphoreType.DMA((4, spread - 1)),
            pltpu.SemaphoreType.DMA((4, spread)),
            pltpu.SemaphoreType.DMA((4, spread - 1)),
            pltpu.SemaphoreType.DMA((4, spread)),
            pltpu.SemaphoreType.DMA((ROUNDS, most - 1)),
            pltpu.SemaphoreType.DMA((ROUNDS, most)),
            pltpu.VMEM((leaves, RANK, LEAF), bf16),
            pltpu.VMEM((leaves - 1, RANK, 2 * RANK), bf16),
        ],
        compiler_params=pltpu.CompilerParams(
            collective_id=0, has_side_effects=True, vmem_limit_bytes=56 * 1024 * 1024
        ),
        name="ridge",
    )(
        targets,
        points,
        tree_order.reshape(-1, RANK),
        leaf_basis,
        transfer_local,
        coupling_local,
        transfer_top.transpose(0, 2, 1),
        coupling_top.transpose(0, 2, 1),
    )
    return pl.pallas_call(
        hand_out,
        out_shape=(out, out),
        in_specs=[hbm_space, hbm_space],
        out_specs=(hbm_space, hbm_space),
        scratch_shapes=[pltpu.VMEM((2, columns, here), f32), pltpu.SemaphoreType.DMA((4,))],
        name="hand_out",
    )(*results)


def solution(mesh):
    placed = (
        P("rhs", "leaf"),
        P(None, "leaf"),
        P("leaf"),
        P("leaf", None, None),
        P("leaf", None, None),
        P("leaf", None, None),
        P(None, None, "rhs"),
        P(None, None, "rhs"),
    )
    return jax.shard_map(
        per_device,
        mesh=mesh,
        in_specs=placed,
        out_specs=(P("rhs", "leaf"), P("rhs", "leaf")),
        check_vma=False,
    )
```
